512 devices in a mesh: batch: 16 (over y, x_lo, core), feat: 32 (over z, x_hi).
Axes of the slice: x: 4 (x_hi: 2, x_lo: 2; x = x_hi * 2 + x_lo), y: 4, z: 16, core: 2. Of those that a mesh axis runs over, the one named last changes fastest.
Arguments:
- first_view: bfloat16 [1024, 8192], P('batch'), may hold values from -16 to 16
- second_view: bfloat16 [1024, 8192], P('batch'), may hold values from -16 to 16
- weight: bfloat16 [8192, 8192], P('batch', 'feat'), may hold values from -0.0625 to 0.0625
Outputs:
- weight_grad: float32 [8192, 8192], P('batch', 'feat')
The draws below stay inside these ranges and needn't reach their ends.
All inputs are finite; a program needn't handle non-finite values.
Results may differ from the reference program's by a relative error of at most 0.03.
Values may be sent and summed in bfloat16 or wider, within the bound.
A program may use at most 64 MiB of HBM per device.

```python
import jax
import jax.numpy as jnp
from jax import lax

D = 8192
ROWS_DEV = 64
ROWS = 1024
N_BATCH = 16


def shared_normal(key):
    return jax.random.normal(key, (ROWS, D), jnp.float32)


def shared_scale(key):
    scale_key = jax.random.fold_in(key, 7)
    jitter = jnp.exp(jax.random.uniform(scale_key, (ROWS, 1), jnp.float32, -0.35, 0.35))
    position = jnp.arange(ROWS, dtype=jnp.float32)[:, None] / ROWS
    return jitter * 3.0 ** position


def draw_first_view(key, part):
    base = shared_normal(key)
    scale = shared_scale(key)
    key = jax.random.fold_in(key, 11)
    noise = jax.random.normal(key, (ROWS, D), jnp.float32)
    return jnp.clip((base + 0.35 * noise) * scale, -16.0, 16.0).astype(jnp.bfloat16)


def draw_second_view(key, part):
    base = shared_normal(key)
    scale = shared_scale(key)
    key = jax.random.fold_in(key, 23)
    noise = jax.random.normal(key, (ROWS, D), jnp.float32)
    return jnp.clip((base + 0.35 * noise) * scale, -16.0, 16.0).astype(jnp.bfloat16)


def level_of(stream_key, extent, pieces, low, high):
    def one(dim, shards_of):
        draws = jax.random.uniform(jax.random.fold_in(jax.random.fold_in(stream_key, 6), dim), (shards_of,), jnp.float32, low / len(pieces), high / len(pieces))
        return jnp.repeat(jnp.exp(draws), extent[dim] // shards_of).reshape((-1,) + (1,) * (len(extent) - dim - 1))

    loudness = one(*pieces[0])
    for cut in pieces[1:]:
        loudness = loudness * one(*cut)
    return loudness


def bell_draw(stream_key, dims, scale, most, shards=(), held_as=jnp.bfloat16):
    loudness = level_of(stream_key, dims, shards, -0.22, 0.18) if shards else 1.0
    result = jax.random.normal(stream_key, dims, jnp.float32) * scale * loudness
    return jnp.minimum(jnp.maximum(result, -most), most).astype(held_as)


def setup_inputs(seed: int = 0) -> dict:
    keys = jax.random.split(jax.random.key(seed), 4)
    first_view = draw_first_view(jax.random.fold_in(keys[3], 71), 0)
    second_view = draw_second_view(jax.random.fold_in(keys[3], 71), 0)
    weight = bell_draw(keys[2], (D, D), D ** -0.5, 0.0625, ((0, 16), (1, 32)))
    return dict(first_view=first_view, second_view=second_view, weight=weight)


off_weight = 0.0051

def normalize(values):
    mean = lax.optimization_barrier(jnp.sum(values, 0)) / ROWS
    spread = lax.optimization_barrier(jnp.sum(values * values, 0)) / ROWS - mean * mean
    scale = lax.rsqrt(spread + 1e-05)
    return (((values - mean) * scale).astype(jnp.bfloat16), scale)

def norm_backward(grad_normed, normed, scale):
    normed_wide = normed.astype(jnp.float32)
    centered = grad_normed - lax.optimization_barrier(jnp.mean(grad_normed, 0)) - normed_wide * lax.optimization_barrier(jnp.mean(grad_normed * normed_wide, 0))
    return (centered * scale).astype(jnp.bfloat16)

def blockwise(left, right):
    block = D // N_BATCH

    def add_block(total, number):
        start = (number * block).astype(jnp.int32)
        left_part = lax.dynamic_slice_in_dim(left, start, block, 1)
        right_part = lax.dynamic_slice_in_dim(right, start, block, 0)
        term = jnp.dot(left_part, right_part, preferred_element_type=jnp.float32) / ROWS
        rounded = lax.optimization_barrier(term.astype(jnp.bfloat16))
        return (total + rounded.astype(jnp.float32), None)
    start_total = jnp.zeros((left.shape[0], right.shape[1]), jnp.float32)
    total, unused = lax.scan(add_block, start_total, jnp.arange(N_BATCH, dtype=jnp.int32))
    return total

def reference(first_view, second_view, weight):
    first_out = jnp.dot(first_view, weight, preferred_element_type=jnp.float32)
    second_out = jnp.dot(second_view, weight, preferred_element_type=jnp.float32)
    first_normed, first_scale = normalize(first_out)
    second_normed, second_scale = normalize(second_out)
    corr = jnp.dot(first_normed.T, second_normed, preferred_element_type=jnp.float32) / ROWS
    index = jnp.arange(D, dtype=jnp.int32)
    ondiag = index[:, None] == index[None, :]
    slope = jnp.where(ondiag, -2.0 * (1.0 - corr), 2.0 * off_weight * corr).astype(jnp.bfloat16)
    first_grad = blockwise(second_normed, slope.T)
    second_grad = blockwise(first_normed, slope)
    first_dz = norm_backward(first_grad, first_normed, first_scale)
    second_dz = norm_backward(second_grad, second_normed, second_scale)
    weight_grad = jnp.dot(first_view.T, first_dz, preferred_element_type=jnp.float32)
    weight_grad = weight_grad + jnp.dot(second_view.T, second_dz, preferred_element_type=jnp.float32)
    return weight_grad * ROWS_DEV
```

```python
import functools

import jax
import jax.numpy as jnp
from jax import lax
from jax.experimental import pallas as pl
from jax.experimental.pallas import tpu as pltpu
from jax.sharding import PartitionSpec as P

MESH = pl.DeviceIdType.MESH
off_weight = 0.0051
NX, NY, NZ = 4, 4, 16
ROWS = 1024
BLOCK = 512
SLAB = 256
PAIR = 2 * BLOCK
PAIRS = 8
OWN = SLAB // PAIRS
STRIP = ROWS // (NX * NY)
BF = jnp.bfloat16
F32 = jnp.float32

ROW_DIMS = (((1,), (1,)), ((), ()))


def coords():
    b = lax.axis_index("batch")
    f = lax.axis_index("feat")
    return (f % 2) * 2 + (b // 2) % 2, b // 4, f // 2, b % 2


def dev(x, y, z, core):
    return ((y * 2 + x % 2) * 2 + core, z * 2 + x // 2)


def rcopy(src, dst, send, recv, device):
    return pltpu.make_async_remote_copy(
        src_ref=src, dst_ref=dst, send_sem=send, recv_sem=recv, device_id=device, device_id_type=MESH
    )


def kernel(
    first, second, w, out,
    xb, xt, wb, wt, pt, ptb, rsb, nt, sc, scb, noth, kl, kp, zb, ks, kf, gs, gb, nn, no, gw, cb, fs, fr,
    loc, x_s, x_r, w_s, w_r, rs_s, rs_r, ag_s, ag_r, sc_s, sc_r, n_s, n_r, zr_s, zr_r, za_s, za_r, g_s, g_r, f_s, f_r,
):
    x, y, z, core = coords()
    xlo, xhi = x % 2, x // 2
    pair = y * 2 + xlo
    place = y * NX + x
    sib = dev(x, y, z, 1 - core)

    barrier = pltpu.get_barrier_semaphore()
    pl.semaphore_signal(barrier, 1, device_id=sib, device_id_type=MESH)

    @pl.loop(1, NX * NY)
    def _(i):
        for c in range(2):
            pl.semaphore_signal(
                barrier, 1, device_id=dev((x + i % NX) % NX, (y + i // NX) % NY, z, c), device_id_type=MESH
            )

    @pl.loop(1, NZ)
    def _(i):
        for c in range(2):
            pl.semaphore_signal(barrier, 1, device_id=dev(x, y, (z + i) % NZ, c), device_id_type=MESH)

    pl.semaphore_wait(barrier, 1 + 2 * (NX * NY - 1) + 2 * (NZ - 1))

    mine = pair * 2 + core

    def x_copy(view, dy, dlo, target):
        ty = (y + dy) % NY
        tlo = (xlo + dlo) % 2
        tx = x if dlo == 0 else (x ^ 1 if view == 0 else 3 - x)
        src = (first, second)[view]
        col = pl.multiple_of((ty * 2 + tlo) * PAIR, PAIR)
        return rcopy(
            src.at[:, pl.ds(col, PAIR)],
            xb.at[pl.ds(pl.multiple_of(mine * 64, 64), 64), :],
            x_s.at[(dy * 2 + dlo) * 2 + view],
            x_r.at[mine],
            dev(tx, ty, z, view) if target is None else target,
        )

    def own_copy(view):
        src = (first, second)[view]
        return pltpu.make_async_copy(
            src.at[:, pl.ds(pl.multiple_of(pair * PAIR, PAIR), PAIR)],
            xb.at[pl.ds(pl.multiple_of(mine * 64, 64), 64), :],
            loc.at[0],
        )

    offsets = [(dy, dlo) for dy in (2, 1, 3, 0) for dlo in (1, 0) if (dy, dlo) != (0, 0)]
    for dy, dlo in offsets:
        for view in range(2):
            x_copy(view, dy, dlo, None).start()
    for view in range(2):
        @pl.when(core == view)
        def _():
            own_copy(view).start()

        @pl.when(core != view)
        def _():
            x_copy(view, 0, 0, sib).start()

    w_place = wb.at[pl.ds(pl.multiple_of(core * BLOCK, BLOCK), BLOCK), :]
    w_copy = rcopy(w, w_place, w_s, w_r, sib)
    w_copy.start()
    w_own = pltpu.make_async_copy(w, w_place, loc.at[1])
    w_own.start()
    w_own.wait()
    w_copy.wait()
    for i in range(PAIR // SLAB):
        wt[:, i * SLAB:(i + 1) * SLAB] = wb[i * SLAB:(i + 1) * SLAB, :].T
    for view in range(2):
        @pl.when(core == view)
        def _():
            own_copy(view).wait()

    def chunk_step(dy, dlo):
        chunk = ((y + dy) % NY) * 2 + (xlo + dlo) % 2
        for c in range(2):
            b = chunk * 2 + c
            rows = pl.ds(pl.multiple_of(b * 64, 64), 64)

            @pl.when(b != mine)
            def _():
                rcopy(xb.at[rows, :], xb.at[rows, :], x_s.at[0], x_r.at[b], sib).wait_recv()

        rows = pl.ds(pl.multiple_of(chunk * 128, 128), 128)
        xs = xb[rows, :]
        pt[:, rows] = lax.dot_general(wt[...], xs, ROW_DIMS, preferred_element_type=F32)
        xt[:, rows] = xs.T

    for dy, dlo in [(0, 0), (0, 1), (1, 0), (3, 0), (1, 1), (3, 1), (2, 0), (2, 1)]:
        chunk_step(dy, dlo)

    for i in range(PAIRS):
        part = pt[i * OWN:(i + 1) * OWN, :]
        ptb[i * OWN:(i + 1) * OWN, :] = (part - jnp.mean(part, 1, keepdims=True)).astype(BF)

    def rs_copy(i):
        ty = (y + i // 2) % NY
        tlo = (xlo + i % 2) % 2
        rows = pl.ds(pl.multiple_of((ty * 2 + tlo) * OWN, OWN), OWN)
        return rcopy(
            ptb.at[rows, :], rsb.at[pair], rs_s.at[i], rs_r.at[pair], dev(xhi * 2 + tlo, ty, z, core)
        )

    @pl.loop(1, PAIRS)
    def _(i):
        rs_copy(i).start()

    rsb[pair] = ptb[pl.ds(pl.multiple_of(pair * OWN, OWN), OWN), :]

    @pl.loop(1, PAIRS)
    def _(i):
        other = (pair + i) % PAIRS
        rcopy(rsb.at[other], rsb.at[other], rs_s.at[0], rs_r.at[other], sib).wait_recv()

    total = rsb[0].astype(F32)
    for i in range(1, PAIRS):
        total = total + rsb[i].astype(F32)
    mean = jnp.sum(total, 1, keepdims=True) / ROWS
    spread = jnp.sum(total * total, 1, keepdims=True) / ROWS - mean * mean
    scale = lax.rsqrt(spread + 1e-05)
    own_rows = pl.ds(pl.multiple_of(xhi * SLAB + pair * OWN, OWN), OWN)
    nt[own_rows, :] = ((total - mean) * scale).astype(BF)
    lane = lax.broadcasted_iota(jnp.int32, (8, 128), 1)
    wide = jnp.broadcast_to(scale, (OWN, 128))
    tile = wide[0:8]
    for i in range(1, OWN // 8):
        tile = jnp.where(lane >= 32 * i, wide[8 * i:8 * i + 8], tile)
    sc[pair] = tile

    def ag_copy(i):
        return rcopy(
            nt.at[own_rows, :], nt.at[own_rows, :], ag_s.at[i], ag_r.at[place],
            dev((x + i % NX) % NX, (y + i // NX) % NY, z, core),
        )

    def sc_copy(i):
        return rcopy(
            sc.at[pair], sc.at[pair], sc_s.at[i], sc_r.at[pair],
            dev(xhi * 2 + (xlo + i % 2) % 2, (y + i // 2) % NY, z, core),
        )

    @pl.loop(1, NX * NY)
    def _(i):
        ag_copy(i).start()

    @pl.loop(1, PAIRS)
    def _(i):
        sc_copy(i).start()

    @pl.loop(1, NX * NY)
    def _(i):
        sx, sy = (x + i % NX) % NX, (y + i // NX) % NY
        rows = pl.ds(pl.multiple_of((sx // 2) * SLAB + (sy * 2 + sx % 2) * OWN, OWN), OWN)
        rcopy(nt.at[rows, :], nt.at[rows, :], ag_s.at[0], ag_r.at[sy * NX + sx], sib).wait_recv()

    kl[...] = nt[:, pl.ds(pl.multiple_of((place // 2) * 128, 128), 128)].T
    strip = kl[pl.ds(pl.multiple_of((place % 2) * STRIP, STRIP), STRIP), :]
    for i in range(4):
        kp[:, i * 256:(i + 1) * 256] = jnp.dot(
            strip, nt[:, i * 256:(i + 1) * 256], preferred_element_type=F32
        ).astype(BF)

    def piece(ref, t):
        return ref.at[pl.ds(pl.multiple_of((t // 4) * 16, 16), 16), pl.ds(pl.multiple_of((t % 4) * 256, 256), 256)]

    def zr_copy(i):
        t = (z + i) % NZ
        return rcopy(piece(kp, t), zb.at[z], zr_s.at[i], zr_r.at[z], dev(x, y, t, core))

    @pl.loop(1, NZ)
    def _(i):
        zr_copy(i).start()

    slab_rows = pl.ds(pl.multiple_of(xhi * SLAB, SLAB), SLAB)
    n_copy = rcopy(nt.at[slab_rows, :], noth, n_s, n_r, sib)
    n_copy.start()

    zb[z] = kp[
        pl.ds(pl.multiple_of((z // 4) * 16, 16), 16), pl.ds(pl.multiple_of((z % 4) * 256, 256), 256)
    ]

    @pl.loop(1, NZ)
    def _(i):
        t = (z + i) % NZ
        rcopy(zb.at[t], zb.at[t], zr_s.at[0], zr_r.at[t], sib).wait_recv()

    acc = zb[0].astype(F32)
    for i in range(1, NZ):
        acc = acc + zb[i].astype(F32)
    ks[...] = acc.astype(BF)

    def za_copy(i):
        return rcopy(ks, piece(kf, z), za_s.at[i], za_r.at[z], dev(x, y, (z + i) % NZ, 1 - core))

    @pl.loop(0, NZ)
    def _(i):
        za_copy(i).start()

    n_copy.wait()
    for i in range(8):
        rows = slice(i * 128, (i + 1) * 128)
        nn[rows, :] = nt[slab_rows, rows].T
        no[rows, :] = noth[:, rows].T
    diag = jnp.zeros((1, SLAB), F32)
    for i in range(8):
        rows = slice(i * 128, (i + 1) * 128)
        diag = diag + jnp.sum(nn[rows, :].astype(F32) * no[rows, :].astype(F32), 0, keepdims=True)
    diag = diag / ROWS
    d = -2.0 * (1.0 - diag) - 2.0 * off_weight * diag

    @pl.loop(1, PAIRS)
    def _(i):
        other = (pair + i) % PAIRS
        rcopy(sc.at[other], sc.at[other], sc_s.at[0], sc_r.at[other], sib).wait_recv()

    cols = []
    for i in range(PAIRS):
        t = sc[i]
        for j in range(OWN // 8):
            cols.append(jnp.broadcast_to(t[:, 32 * j:32 * j + 1], (8, 128)))
    scale_row = jnp.concatenate(cols, 0).T[0:1, :]

    @pl.loop(0, NZ)
    def _(i):
        t = (z + i) % NZ
        rcopy(ks, piece(kf, t), za_s.at[0], za_r.at[t], sib).wait_recv()

    for h in range(2):
        gs[h] = lax.dot_general(
            kf[...], nt[h * SLAB:(h + 1) * SLAB, :], ROW_DIMS, preferred_element_type=F32
        ).astype(BF)

    def g_copy(i):
        tx = (x + i % NX) % NX
        return rcopy(
            gs.at[tx // 2], gb.at[pl.ds(pl.multiple_of(place * STRIP, STRIP), STRIP), :], g_s.at[i], g_r.at[place],
            dev(tx, (y + i // NX) % NY, z, core),
        )

    @pl.loop(1, NX * NY)
    def _(i):
        g_copy(i).start()

    gb[pl.ds(pl.multiple_of(place * STRIP, STRIP), STRIP), :] = gs[xhi]

    @pl.loop(1, NX * NY)
    def _(i):
        t = ((y + i // NX) % NY) * NX + (x + i % NX) % NX
        rows = pl.ds(pl.multiple_of(t * STRIP, STRIP), STRIP)
        rcopy(gb.at[rows, :], gb.at[rows, :], g_s.at[0], g_r.at[t], sib).wait_recv()

    g_sum = jnp.zeros((1, SLAB), F32)
    gn_sum = jnp.zeros((1, SLAB), F32)
    for i in range(8):
        rows = slice(i * 128, (i + 1) * 128)
        g = gb[rows, :].astype(F32) * (2.0 * off_weight / ROWS) + no[rows, :].astype(F32) * d
        gw[rows, :] = g
        g_sum = g_sum + jnp.sum(g, 0, keepdims=True)
        gn_sum = gn_sum + jnp.sum(g * nn[rows, :].astype(F32), 0, keepdims=True)
    g_mean = g_sum / ROWS
    gn_mean = gn_sum / ROWS
    for i in range(8):
        rows = slice(i * 128, (i + 1) * 128)
        cb[rows, :] = (gw[rows, :] - g_mean - nn[rows, :].astype(F32) * gn_mean).astype(BF)

    factor = scale_row * (64.0 / ROWS)

    def product(block, i):
        rows = pl.ds(pl.multiple_of(block * BLOCK + i * 128, 128), 128)
        return jnp.dot(xt[rows, :], cb[...], preferred_element_type=F32) * factor

    for i in range(4):
        fs[i * 128:(i + 1) * 128, :] = product(1 - core, i)
    f_copy = rcopy(fs, fr, f_s, f_r, sib)
    f_copy.start()
    for i in range(4):
        out[i * 128:(i + 1) * 128, :] = product(core, i)
    f_copy.wait()
    out[...] += fr[...]

    for dy, dlo in offsets:
        for view in range(2):
            x_copy(view, dy, dlo, None).wait_send()
    for view in range(2):
        @pl.when(core != view)
        def _():
            x_copy(view, 0, 0, sib).wait_send()

    @pl.loop(1, PAIRS)
    def _(i):
        rs_copy(i).wait_send()
        sc_copy(i).wait_send()

    @pl.loop(1, NX * NY)
    def _(i):
        ag_copy(i).wait_send()
        g_copy(i).wait_send()

    @pl.loop(1, NZ)
    def _(i):
        zr_copy(i).wait_send()

    @pl.loop(0, NZ)
    def _(i):
        za_copy(i).wait_send()


def local(first_view, second_view, weight):
    dma = pltpu.SemaphoreType.DMA
    vm = pltpu.VMEM
    return pl.pallas_call(
        kernel,
        out_shape=jax.ShapeDtypeStruct((BLOCK, SLAB), F32),
        in_specs=[pl.BlockSpec(memory_space=pl.ANY)] * 3,
        out_specs=pl.BlockSpec(memory_space=pltpu.VMEM),
        scratch_shapes=[
            vm((ROWS, PAIR), BF), vm((PAIR, ROWS), BF), vm((PAIR, SLAB), BF), vm((SLAB, PAIR), BF),
            vm((SLAB, ROWS), F32), vm((SLAB, ROWS), BF), vm((PAIRS, OWN, ROWS), BF), vm((2 * SLAB, ROWS), BF),
            vm((PAIRS, 8, 128), F32), vm((8, 128), F32), vm((SLAB, ROWS), BF), vm((128, 2 * SLAB), BF),
            vm((STRIP, ROWS), BF), vm((NZ, 16, 256), BF), vm((16, 256), BF), vm((STRIP, ROWS), BF),
            vm((2, STRIP, SLAB), BF), vm((ROWS, SLAB), BF), vm((ROWS, SLAB), BF), vm((ROWS, SLAB), BF),
            vm((ROWS, SLAB), F32), vm((ROWS, SLAB), BF), vm((BLOCK, SLAB), F32), vm((BLOCK, SLAB), F32),
            dma((2,)), dma((16,)), dma((16,)), dma, dma, dma((PAIRS,)), dma((PAIRS,)), dma((16,)), dma((16,)),
            dma((PAIRS,)), dma((PAIRS,)), dma, dma, dma((NZ,)), dma((NZ,)), dma((NZ,)), dma((NZ,)),
            dma((16,)), dma((16,)), dma, dma,
        ],
        compiler_params=pltpu.CompilerParams(collective_id=0, has_side_effects=True, vmem_limit_bytes=48 << 20),
        cost_estimate=pl.CostEstimate(flops=4 * 10**9, bytes_accessed=4 << 20, transcendentals=0),
    )(first_view, second_view, weight)


def solution(mesh):
    return jax.shard_map(
        local,
        mesh=mesh,
        in_specs=(P("batch", None), P("batch", None), P("batch", "feat")),
        out_specs=P("batch", "feat"),
        check_vma=False,
    )
```

```python
import functools

import jax
import jax.numpy as jnp
from jax import lax
from jax.experimental import pallas as pl
from jax.experimental.pallas import tpu as pltpu
from jax.sharding import PartitionSpec as P

MESH = pl.DeviceIdType.MESH
off_weight = 0.0051
NX, NY, NZ = 4, 4, 16
ROWS = 1024
BLOCK = 512
SLAB = 256
PAIR = 2 * BLOCK
PAIRS = 8
OWN = SLAB // PAIRS
STRIP = ROWS // (NX * NY)
BF = jnp.bfloat16
F32 = jnp.float32

ROW_DIMS = (((1,), (1,)), ((), ()))


def coords():
    b = lax.axis_index("batch")
    f = lax.axis_index("feat")
    return (f & 1) * 2 + ((b >> 1) & 1), b >> 2, f >> 1, b & 1


def dev(x, y, z, core):
    return (y * 4 + (x & 1) * 2 + core, z * 2 + (x >> 1))


def each(low, high):
    def run(body):
        for i in range(low, high):
            body(i)

    return run


def rcopy(src, dst, send, recv, device):
    return pltpu.make_async_remote_copy(
        src_ref=src, dst_ref=dst, send_sem=send, recv_sem=recv, device_id=device, device_id_type=MESH
    )


def kernel(
    first, second, w, out,
    xb, xt, wb, wt, pt, ptb, rsb, nt, sc, scb, noth, kl, kp, zb, ks, kf, gs, gb, nn, no, gw, cb, fs, fr,
    loc, x_s, x_r, w_s, w_r, rs_s, rs_r, ag_s, ag_r, sc_s, sc_r, n_s, n_r, zr_s, zr_r, za_s, za_r, g_s, g_r, f_s, f_r,
):
    x, y, z, core = coords()
    xlo, xhi = x & 1, x >> 1
    pair = y * 2 + xlo
    place = y * NX + x
    sib = dev(x, y, z, 1 - core)
    sent = []

    def when_sent(copy, low, high):
        def wait():
            @each(low, high)
            def _(i):
                copy(i).wait_send()

        sent.append(wait)

    barrier = pltpu.get_barrier_semaphore()
    pl.semaphore_signal(barrier, 1, device_id=sib, device_id_type=MESH)

    @each(1, NX * NY)
    def _(i):
        for c in range(2):
            pl.semaphore_signal(
                barrier, 1, device_id=dev((x + i) & 3, (y + (i >> 2)) & 3, z, c), device_id_type=MESH
            )

    @each(1, NZ)
    def _(i):
        for c in range(2):
            pl.semaphore_signal(barrier, 1, device_id=dev(x, y, (z + i) & 15, c), device_id_type=MESH)

    pl.semaphore_wait(barrier, 1 + 2 * (NX * NY - 1) + 2 * (NZ - 1))

    mine = pair * 2 + core

    def x_copy(view, dy, dlo, target):
        ty = (y + dy) & 3
        tlo = (xlo ^ dlo)
        tx = x if dlo == 0 else (x ^ 1 if view == 0 else 3 - x)
        src = (first, second)[view]
        col = pl.multiple_of((ty * 2 + tlo) * PAIR, PAIR)
        return rcopy(
            src.at[:, pl.ds(col, PAIR)],
            xb.at[pl.ds(pl.multiple_of(mine * 64, 64), 64), :],
            x_s.at[(dy * 2 + dlo) * 2 + view],
            x_r.at[mine],
            dev(tx, ty, z, view) if target is None else target,
        )

    def own_copy(view):
        src = (first, second)[view]
        return pltpu.make_async_copy(
            src.at[:, pl.ds(pl.multiple_of(pair * PAIR, PAIR), PAIR)],
            xb.at[pl.ds(pl.multiple_of(mine * 64, 64), 64), :],
            loc.at[0],
        )

    offsets = [(dy, dlo) for dy in (2, 1, 3, 0) for dlo in (1, 0) if (dy, dlo) != (0, 0)]
    for dy, dlo in offsets:
        for view in range(2):
            x_copy(view, dy, dlo, None).start()
    for view in range(2):
        @pl.when(core == view)
        def _():
            own_copy(view).start()

        @pl.when(core != view)
        def _():
            x_copy(view, 0, 0, sib).start()

    def x_sent():
        for dy, dlo in offsets:
            for view in range(2):
                x_copy(view, dy, dlo, None).wait_send()
        for view in range(2):
            @pl.when(core != view)
            def _():
                x_copy(view, 0, 0, sib).wait_send()

    sent.append(x_sent)

    w_place = wb.at[pl.ds(pl.multiple_of(core * BLOCK, BLOCK), BLOCK), :]
    w_copy = rcopy(w, w_place, w_s, w_r, sib)
    w_copy.start()
    w_own = pltpu.make_async_copy(w, w_place, loc.at[1])
    w_own.start()
    w_own.wait()
    w_copy.wait()
    for i in range(PAIR // SLAB):
        wt[:, i * SLAB:(i + 1) * SLAB] = wb[i * SLAB:(i + 1) * SLAB, :].T
    for view in range(2):
        @pl.when(core == view)
        def _():
            own_copy(view).wait()

    def chunk_step(dy, dlo):
        chunk = ((y + dy) & 3) * 2 + (xlo ^ dlo)
        for c in range(2):
            b = chunk * 2 + c
            rows = pl.ds(pl.multiple_of(b * 64, 64), 64)

            @pl.when(b != mine)
            def _():
                rcopy(xb.at[rows, :], xb.at[rows, :], x_s.at[0], x_r.at[b], sib).wait_recv()

        rows = pl.ds(pl.multiple_of(chunk * 128, 128), 128)
        xs = xb[rows, :]
        pt[:, rows] = lax.dot_general(wt[...], xs, ROW_DIMS, preferred_element_type=F32)
        xt[:, rows] = xs.T

    for dy, dlo in [(0, 0), (0, 1), (1, 0), (3, 0), (1, 1), (3, 1), (2, 0), (2, 1)]:
        chunk_step(dy, dlo)

    for i in range(PAIRS):
        part = pt[i * OWN:(i + 1) * OWN, :]
        ptb[i * OWN:(i + 1) * OWN, :] = (part - jnp.mean(part, 1, keepdims=True)).astype(BF)

    def rs_copy(i):
        ty = (y + (i >> 1)) & 3
        tlo = xlo ^ (i & 1)
        rows = pl.ds(pl.multiple_of((ty * 2 + tlo) * OWN, OWN), OWN)
        return rcopy(
            ptb.at[rows, :], rsb.at[pair], rs_s.at[i], rs_r.at[pair], dev(xhi * 2 + tlo, ty, z, core)
        )

    @each(1, PAIRS)
    def _(i):
        rs_copy(i).start()

    when_sent(rs_copy, 1, PAIRS)

    rsb[pair] = ptb[pl.ds(pl.multiple_of(pair * OWN, OWN), OWN), :]

    @each(1, PAIRS)
    def _(i):
        other = (pair + i) & 7
        rcopy(rsb.at[other], rsb.at[other], rs_s.at[0], rs_r.at[other], sib).wait_recv()

    total = rsb[0].astype(F32)
    for i in range(1, PAIRS):
        total = total + rsb[i].astype(F32)
    mean = jnp.sum(total, 1, keepdims=True) / ROWS
    spread = jnp.sum(total * total, 1, keepdims=True) / ROWS - mean * mean
    scale = lax.rsqrt(spread + 1e-05)
    own_rows = pl.ds(pl.multiple_of(xhi * SLAB + pair * OWN, OWN), OWN)
    nt[own_rows, :] = ((total - mean) * scale).astype(BF)
    lane = lax.broadcasted_iota(jnp.int32, (8, 128), 1)
    wide = jnp.broadcast_to(scale, (OWN, 128))
    tile = wide[0:8]
    for i in range(1, OWN // 8):
        tile = jnp.where(lane >= 32 * i, wide[8 * i:8 * i + 8], tile)
    sc[pair] = tile

    def ag_copy(i):
        return rcopy(
            nt.at[own_rows, :], nt.at[own_rows, :], ag_s.at[i], ag_r.at[place],
            dev((x + i) & 3, (y + (i >> 2)) & 3, z, core),
        )

    def sc_copy(i):
        return rcopy(
            sc.at[pair], sc.at[pair], sc_s.at[i], sc_r.at[pair],
            dev(xhi * 2 + xlo ^ (i & 1), (y + (i >> 1)) & 3, z, core),
        )

    @each(1, NX * NY)
    def _(i):
        ag_copy(i).start()

    when_sent(ag_copy, 1, NX * NY)

    @each(1, PAIRS)
    def _(i):
        sc_copy(i).start()

    when_sent(sc_copy, 1, PAIRS)

    @each(1, NX * NY)
    def _(i):
        sx, sy = (x + i) & 3, (y + (i >> 2)) & 3
        rows = pl.ds(pl.multiple_of((sx >> 1) * SLAB + (sy * 2 + (sx & 1)) * OWN, OWN), OWN)
        rcopy(nt.at[rows, :], nt.at[rows, :], ag_s.at[0], ag_r.at[sy * NX + sx], sib).wait_recv()

    @each(1, PAIRS)
    def _(i):
        other = (pair + i) & 7
        rcopy(sc.at[other], sc.at[other], sc_s.at[0], sc_r.at[other], sib).wait_recv()

    kl[...] = nt[:, pl.ds(pl.multiple_of((place >> 1) * 128, 128), 128)].T
    strip = kl[pl.ds(pl.multiple_of((place & 1) * STRIP, STRIP), STRIP), :]
    for i in range(4):
        kp[:, i * 256:(i + 1) * 256] = jnp.dot(
            strip, nt[:, i * 256:(i + 1) * 256], preferred_element_type=F32
        ).astype(BF)

    def piece(ref, t):
        return ref.at[pl.ds(pl.multiple_of((t >> 2) * 16, 16), 16), pl.ds(pl.multiple_of((t & 3) * 256, 256), 256)]

    def zr_copy(i):
        t = (z + i) & 15
        return rcopy(piece(kp, t), zb.at[z], zr_s.at[i], zr_r.at[z], dev(x, y, t, core))

    @each(1, NZ)
    def _(i):
        zr_copy(i).start()

    when_sent(zr_copy, 1, NZ)

    slab_rows = pl.ds(pl.multiple_of(xhi * SLAB, SLAB), SLAB)
    n_copy = rcopy(nt.at[slab_rows, :], noth, n_s, n_r, sib)
    n_copy.start()

    zb[z] = kp[
        pl.ds(pl.multiple_of((z >> 2) * 16, 16), 16), pl.ds(pl.multiple_of((z & 3) * 256, 256), 256)
    ]

    @each(1, NZ)
    def _(i):
        t = (z + i) & 15
        rcopy(zb.at[t], zb.at[t], zr_s.at[0], zr_r.at[t], sib).wait_recv()

    n_copy.wait()
    acc = zb[0].astype(F32)
    for i in range(1, NZ):
        acc = acc + zb[i].astype(F32)
    ks[...] = acc.astype(BF)

    def za_copy(i):
        return rcopy(ks, piece(kf, z), za_s.at[i], za_r.at[z], dev(x, y, (z + i) & 15, 1 - core))

    @each(0, NZ)
    def _(i):
        za_copy(i).start()

    when_sent(za_copy, 0, NZ)

    for i in range(8):
        rows = slice(i * 128, (i + 1) * 128)
        nn[rows, :] = nt[slab_rows, rows].T
        no[rows, :] = noth[:, rows].T
    diag = jnp.zeros((1, SLAB), F32)
    for i in range(8):
        rows = slice(i * 128, (i + 1) * 128)
        diag = diag + jnp.sum(nn[rows, :].astype(F32) * no[rows, :].astype(F32), 0, keepdims=True)
    diag = diag / ROWS
    d = -2.0 * (1.0 - diag) - 2.0 * off_weight * diag

    cols = []
    for i in range(PAIRS):
        t = sc[i]
        for j in range(OWN // 8):
            cols.append(jnp.broadcast_to(t[:, 32 * j:32 * j + 1], (8, 128)))
    scale_row = jnp.concatenate(cols, 0).T[0:1, :]

    @each(0, NZ)
    def _(i):
        t = (z + i) & 15
        rcopy(ks, piece(kf, t), za_s.at[0], za_r.at[t], sib).wait_recv()

    for h in range(2):
        gs[h] = lax.dot_general(
            kf[...], nt[h * SLAB:(h + 1) * SLAB, :], ROW_DIMS, preferred_element_type=F32
        ).astype(BF)

    def g_copy(i):
        tx = (x + i) & 3
        return rcopy(
            gs.at[tx >> 1], gb.at[pl.ds(pl.multiple_of(place * STRIP, STRIP), STRIP), :], g_s.at[i], g_r.at[place],
            dev(tx, (y + (i >> 2)) & 3, z, core),
        )

    @each(1, NX * NY)
    def _(i):
        g_copy(i).start()

    when_sent(g_copy, 1, NX * NY)

    gb[pl.ds(pl.multiple_of(place * STRIP, STRIP), STRIP), :] = gs[xhi]

    @each(1, NX * NY)
    def _(i):
        t = ((y + (i >> 2)) & 3) * NX + ((x + i) & 3)
        rows = pl.ds(pl.multiple_of(t * STRIP, STRIP), STRIP)
        rcopy(gb.at[rows, :], gb.at[rows, :], g_s.at[0], g_r.at[t], sib).wait_recv()

    g_sum = jnp.zeros((1, SLAB), F32)
    gn_sum = jnp.zeros((1, SLAB), F32)
    for i in range(8):
        rows = slice(i * 128, (i + 1) * 128)
        g = gb[rows, :].astype(F32) * (2.0 * off_weight / ROWS) + no[rows, :].astype(F32) * d
        gw[rows, :] = g
        g_sum = g_sum + jnp.sum(g, 0, keepdims=True)
        gn_sum = gn_sum + jnp.sum(g * nn[rows, :].astype(F32), 0, keepdims=True)
    g_mean = g_sum / ROWS
    gn_mean = gn_sum / ROWS
    for i in range(8):
        rows = slice(i * 128, (i + 1) * 128)
        cb[rows, :] = (gw[rows, :] - g_mean - nn[rows, :].astype(F32) * gn_mean).astype(BF)

    factor = scale_row * (64.0 / ROWS)

    def product(block, i):
        rows = pl.ds(pl.multiple_of(block * BLOCK + i * 128, 128), 128)
        return jnp.dot(xt[rows, :], cb[...], preferred_element_type=F32) * factor

    for i in range(4):
        fs[i * 128:(i + 1) * 128, :] = product(1 - core, i)
    f_copy = rcopy(fs, fr, f_s, f_r, sib)
    f_copy.start()
    for i in range(4):
        out[i * 128:(i + 1) * 128, :] = product(core, i)
    f_copy.wait()
    out[...] += fr[...]

    for wait in sent:
        wait()


def local(first_view, second_view, weight):
    dma = pltpu.SemaphoreType.DMA
    vm = pltpu.VMEM
    return pl.pallas_call(
        kernel,
        out_shape=jax.ShapeDtypeStruct((BLOCK, SLAB), F32),
        in_specs=[pl.BlockSpec(memory_space=pl.ANY)] * 3,
        out_specs=pl.BlockSpec(memory_space=pltpu.VMEM),
        scratch_shapes=[
            vm((ROWS, PAIR), BF), vm((PAIR, ROWS), BF), vm((PAIR, SLAB), BF), vm((SLAB, PAIR), BF),
            vm((SLAB, ROWS), F32), vm((SLAB, ROWS), BF), vm((PAIRS, OWN, ROWS), BF), vm((2 * SLAB, ROWS), BF),
            vm((PAIRS, 8, 128), F32), vm((8, 128), F32), vm((SLAB, ROWS), BF), vm((128, 2 * SLAB), BF),
            vm((STRIP, ROWS), BF), vm((NZ, 16, 256), BF), vm((16, 256), BF), vm((STRIP, ROWS), BF),
            vm((2, STRIP, SLAB), BF), vm((ROWS, SLAB), BF), vm((ROWS, SLAB), BF), vm((ROWS, SLAB), BF),
            vm((ROWS, SLAB), F32), vm((ROWS, SLAB), BF), vm((BLOCK, SLAB), F32), vm((BLOCK, SLAB), F32),
            dma((2,)), dma((16,)), dma((16,)), dma, dma, dma((PAIRS,)), dma((PAIRS,)), dma((16,)), dma((16,)),
            dma((PAIRS,)), dma((PAIRS,)), dma, dma, dma((NZ,)), dma((NZ,)), dma((NZ,)), dma((NZ,)),
            dma((16,)), dma((16,)), dma, dma,
        ],
        compiler_params=pltpu.CompilerParams(collective_id=0, has_side_effects=True, vmem_limit_bytes=48 << 20),
        cost_estimate=pl.CostEstimate(flops=4 * 10**9, bytes_accessed=4 << 20, transcendentals=0),
    )(first_view, second_view, weight)


def solution(mesh):
    return jax.shard_map(
        local,
        mesh=mesh,
        in_specs=(P("batch", None), P("batch", None), P("batch", "feat")),
        out_specs=P("batch", "feat"),
        check_vma=False,
    )
```

```python
import functools

import jax
import jax.numpy as jnp
from jax import lax
from jax.experimental import pallas as pl
from jax.experimental.pallas import tpu as pltpu
from jax.sharding import PartitionSpec as P

MESH = pl.DeviceIdType.MESH
off_weight = 0.0051
NX, NY, NZ = 4, 4, 16
ROWS = 1024
BLOCK = 512
SLAB = 256
PAIR = 2 * BLOCK
PAIRS = 8
OWN = SLAB // PAIRS
STRIP = ROWS // (NX * NY)
BF = jnp.bfloat16
F32 = jnp.float32

ROW_DIMS = (((1,), (1,)), ((), ()))


def coords():
    b = lax.axis_index("batch")
    f = lax.axis_index("feat")
    return (f & 1) * 2 + ((b >> 1) & 1), b >> 2, f >> 1, b & 1


def dev(x, y, z, core):
    return (y * 4 + (x & 1) * 2 + core, z * 2 + (x >> 1))


def each(values):
    def run(body):
        for i in values:
            body(i)

    return run


def ring(step, size):
    return min(step, size - step)


PLANE_FAR = sorted(range(1, 16), key=lambda i: -ring(i & 3, 4) - ring(i >> 2, 4))
GROUP_FAR = sorted(range(1, PAIRS), key=lambda i: -(i & 1) - ring(i >> 1, 4))
X_ORDER = [(2, 1), (1, 1), (3, 1), (2, 0), (1, 0), (3, 0), (0, 1)]
LINE_FAR = sorted(range(NZ), key=lambda i: -ring(i, NZ))


def rcopy(src, dst, send, recv, device):
    return pltpu.make_async_remote_copy(
        src_ref=src, dst_ref=dst, send_sem=send, recv_sem=recv, device_id=device, device_id_type=MESH
    )


def kernel(
    first, second, w, out,
    xb, xt, wb, wt, pt, ptb, rsb, nt, sc, scb, noth, kl, kp, zb, ks, kf, gs, gb, nn, no, gw, cb, fs, fr,
    loc, x_s, x_r, q_s, q_r, w_s, w_r, rs_s, rs_r, ag_s, ag_r, sc_s, sc_r, n_s, n_r, zr_s, zr_r, za_s, za_r, g_s, g_r, f_s, f_r,
):
    x, y, z, core = coords()
    xlo, xhi = x & 1, x >> 1
    pair = y * 2 + xlo
    place = y * NX + x
    sib = dev(x, y, z, 1 - core)
    sent = []

    def when_sent(copy, values):
        def wait():
            for i in values:
                copy(i).wait_send()

        sent.append(wait)

    barrier = pltpu.get_barrier_semaphore()
    pl.semaphore_signal(barrier, 1, device_id=sib, device_id_type=MESH)

    @each(PLANE_FAR)
    def _(i):
        for c in range(2):
            pl.semaphore_signal(
                barrier, 1, device_id=dev((x + i) & 3, (y + (i >> 2)) & 3, z, c), device_id_type=MESH
            )

    @each(LINE_FAR[:-1])
    def _(i):
        for c in range(2):
            pl.semaphore_signal(barrier, 1, device_id=dev(x, y, (z + i) & 15, c), device_id_type=MESH)

    pl.semaphore_wait(barrier, 1 + 2 * (NX * NY - 1) + 2 * (NZ - 1))

    mine = pair * 2 + core

    half = z & 1

    def half_cols(h):
        return pl.ds(pl.multiple_of(h * BLOCK, BLOCK), BLOCK)

    def batch_rows(b):
        return pl.ds(pl.multiple_of(b * 64, 64), 64)

    def x_copy(view, dy, dlo):
        ty = (y + dy) & 3
        tlo = xlo ^ dlo
        tx = x if dlo == 0 else (x ^ 1 if view == 0 else 3 - x)
        src = (first, second)[view]
        col = pl.multiple_of((ty * 2 + tlo) * PAIR + half * BLOCK, BLOCK)
        return rcopy(
            src.at[:, pl.ds(col, BLOCK)],
            xb.at[batch_rows(mine), half_cols(half)],
            x_s.at[(dy * 2 + dlo) * 2 + view],
            x_r.at[mine],
            dev(tx, ty, z, view),
        )

    def sib_copy(view):
        src = (first, second)[view]
        return rcopy(
            src.at[:, pl.ds(pl.multiple_of(pair * PAIR, PAIR), PAIR)],
            xb.at[batch_rows(mine), :],
            x_s.at[0],
            x_r.at[mine],
            sib,
        )

    def own_copy(view):
        src = (first, second)[view]
        return pltpu.make_async_copy(
            src.at[:, pl.ds(pl.multiple_of(pair * PAIR, PAIR), PAIR)],
            xb.at[batch_rows(mine), :],
            loc.at[0],
        )

    for dy, dlo in X_ORDER:
        for view in range(2):
            x_copy(view, dy, dlo).start()
    for view in range(2):
        @pl.when(core == view)
        def _():
            own_copy(view).start()

        @pl.when(core != view)
        def _():
            sib_copy(view).start()

    def x_sent():
        for dy, dlo in X_ORDER:
            for view in range(2):
                x_copy(view, dy, dlo).wait_send()
        for view in range(2):
            @pl.when(core != view)
            def _():
                sib_copy(view).wait_send()

    sent.append(x_sent)

    w_place = wb.at[pl.ds(pl.multiple_of(core * BLOCK, BLOCK), BLOCK), :]
    w_copy = rcopy(w, w_place, w_s, w_r, sib)
    w_copy.start()
    w_own = pltpu.make_async_copy(w, w_place, loc.at[1])
    w_own.start()
    w_own.wait()
    w_copy.wait()
    for i in range(PAIR // SLAB):
        wt[:, i * SLAB:(i + 1) * SLAB] = wb[i * SLAB:(i + 1) * SLAB, :].T
    def chunk_of(dy, dlo):
        return ((y + dy) & 3) * 2 + (xlo ^ dlo)

    def relay(dy, dlo, c):
        b = chunk_of(dy, dlo) * 2 + c
        place_there = xb.at[batch_rows(b), half_cols(half)]
        return rcopy(
            place_there, place_there, q_s.at[(dy * 2 + dlo) * 2 + c], q_r.at[b],
            dev(x, y, (z + (1 if c == 0 else 15)) & 15, core),
        )

    def product_of(chunk, h, add):
        rows = pl.ds(pl.multiple_of(chunk * 128, 128), 128)
        xs = xb[rows, half_cols(h)]
        part = lax.dot_general(wt[:, half_cols(h)], xs, ROW_DIMS, preferred_element_type=F32)
        pt[:, rows] = pt[:, rows] + part if add else part
        xt[half_cols(h), rows] = xs.T

    for dy, dlo in X_ORDER:
        for c in range(2):
            b = chunk_of(dy, dlo) * 2 + c
            got = xb.at[batch_rows(b), half_cols(half)]
            rcopy(got, got, x_s.at[0], x_r.at[b], sib).wait_recv()
            relay(dy, dlo, c).start()
        product_of(chunk_of(dy, dlo), half, False)

    def relay_sent():
        for dy, dlo in X_ORDER:
            for c in range(2):
                relay(dy, dlo, c).wait_send()

    sent.append(relay_sent)

    for view in range(2):
        @pl.when(core == view)
        def _():
            own_copy(view).wait()
    got = xb.at[batch_rows(pair * 2 + 1 - core), :]
    rcopy(got, got, x_s.at[0], x_r.at[pair * 2 + 1 - core], sib).wait_recv()
    product_of(pair, half, False)
    product_of(pair, 1 - half, True)

    for dy, dlo in X_ORDER:
        for c in range(2):
            b = chunk_of(dy, dlo) * 2 + c
            got = xb.at[batch_rows(b), half_cols(1 - half)]
            rcopy(got, got, q_s.at[0], q_r.at[b], sib).wait_recv()
        product_of(chunk_of(dy, dlo), 1 - half, True)

    for i in range(PAIRS):
        part = pt[i * OWN:(i + 1) * OWN, :]
        ptb[i * OWN:(i + 1) * OWN, :] = (part - jnp.mean(part, 1, keepdims=True)).astype(BF)

    def rs_copy(i):
        ty = (y + (i >> 1)) & 3
        tlo = xlo ^ (i & 1)
        rows = pl.ds(pl.multiple_of((ty * 2 + tlo) * OWN, OWN), OWN)
        return rcopy(
            ptb.at[rows, :], rsb.at[pair], rs_s.at[i], rs_r.at[pair], dev(xhi * 2 + tlo, ty, z, core)
        )

    @each(GROUP_FAR)
    def _(i):
        rs_copy(i).start()

    when_sent(rs_copy, GROUP_FAR)

    rsb[pair] = ptb[pl.ds(pl.multiple_of(pair * OWN, OWN), OWN), :]

    @each(GROUP_FAR)
    def _(i):
        other = (pair + i) & 7
        rcopy(rsb.at[other], rsb.at[other], rs_s.at[0], rs_r.at[other], sib).wait_recv()

    total = rsb[0].astype(F32)
    for i in range(1, PAIRS):
        total = total + rsb[i].astype(F32)
    mean = jnp.sum(total, 1, keepdims=True) / ROWS
    spread = jnp.sum(total * total, 1, keepdims=True) / ROWS - mean * mean
    scale = lax.rsqrt(spread + 1e-05)
    own_rows = pl.ds(pl.multiple_of(xhi * SLAB + pair * OWN, OWN), OWN)
    nt[own_rows, :] = ((total - mean) * scale).astype(BF)
    lane = lax.broadcasted_iota(jnp.int32, (8, 128), 1)
    wide = jnp.broadcast_to(scale, (OWN, 128))
    tile = wide[0:8]
    for i in range(1, OWN // 8):
        tile = jnp.where(lane >= 32 * i, wide[8 * i:8 * i + 8], tile)
    sc[pair] = tile

    def ag_copy(i):
        return rcopy(
            nt.at[own_rows, :], nt.at[own_rows, :], ag_s.at[i], ag_r.at[place],
            dev((x + i) & 3, (y + (i >> 2)) & 3, z, core),
        )

    def sc_copy(i):
        return rcopy(
            sc.at[pair], sc.at[pair], sc_s.at[i], sc_r.at[pair],
            dev(xhi * 2 + xlo ^ (i & 1), (y + (i >> 1)) & 3, z, core),
        )

    @each(PLANE_FAR)
    def _(i):
        ag_copy(i).start()

    when_sent(ag_copy, PLANE_FAR)

    @each(GROUP_FAR)
    def _(i):
        sc_copy(i).start()

    when_sent(sc_copy, GROUP_FAR)

    @each(PLANE_FAR)
    def _(i):
        sx, sy = (x + i) & 3, (y + (i >> 2)) & 3
        rows = pl.ds(pl.multiple_of((sx >> 1) * SLAB + (sy * 2 + (sx & 1)) * OWN, OWN), OWN)
        rcopy(nt.at[rows, :], nt.at[rows, :], ag_s.at[0], ag_r.at[sy * NX + sx], sib).wait_recv()

    @each(GROUP_FAR)
    def _(i):
        other = (pair + i) & 7
        rcopy(sc.at[other], sc.at[other], sc_s.at[0], sc_r.at[other], sib).wait_recv()

    kl[...] = nt[:, pl.ds(pl.multiple_of((place >> 1) * 128, 128), 128)].T
    strip = kl[pl.ds(pl.multiple_of((place & 1) * STRIP, STRIP), STRIP), :]
    for i in range(4):
        kp[:, i * 256:(i + 1) * 256] = jnp.dot(
            strip, nt[:, i * 256:(i + 1) * 256], preferred_element_type=F32
        ).astype(BF)

    def piece(ref, t):
        return ref.at[pl.ds(pl.multiple_of((t >> 2) * 16, 16), 16), pl.ds(pl.multiple_of((t & 3) * 256, 256), 256)]

    def zr_copy(i):
        t = (z + i) & 15
        return rcopy(piece(kp, t), zb.at[z], zr_s.at[i], zr_r.at[z], dev(x, y, t, core))

    @each(LINE_FAR[:-1])
    def _(i):
        zr_copy(i).start()

    when_sent(zr_copy, LINE_FAR[:-1])

    slab_rows = pl.ds(pl.multiple_of(xhi * SLAB, SLAB), SLAB)
    n_copy = rcopy(nt.at[slab_rows, :], noth, n_s, n_r, sib)
    n_copy.start()

    zb[z] = kp[
        pl.ds(pl.multiple_of((z >> 2) * 16, 16), 16), pl.ds(pl.multiple_of((z & 3) * 256, 256), 256)
    ]

    @each(LINE_FAR[:-1])
    def _(i):
        t = (z + i) & 15
        rcopy(zb.at[t], zb.at[t], zr_s.at[0], zr_r.at[t], sib).wait_recv()

    n_copy.wait()
    acc = zb[0].astype(F32)
    for i in range(1, NZ):
        acc = acc + zb[i].astype(F32)
    ks[...] = acc.astype(BF)

    def za_copy(i):
        return rcopy(ks, piece(kf, z), za_s.at[i], za_r.at[z], dev(x, y, (z + i) & 15, 1 - core))

    @each(LINE_FAR)
    def _(i):
        za_copy(i).start()

    when_sent(za_copy, LINE_FAR)

    for i in range(8):
        rows = slice(i * 128, (i + 1) * 128)
        nn[rows, :] = nt[slab_rows, rows].T
        no[rows, :] = noth[:, rows].T
    diag = jnp.zeros((1, SLAB), F32)
    for i in range(8):
        rows = slice(i * 128, (i + 1) * 128)
        diag = diag + jnp.sum(nn[rows, :].astype(F32) * no[rows, :].astype(F32), 0, keepdims=True)
    diag = diag / ROWS
    d = -2.0 * (1.0 - diag) - 2.0 * off_weight * diag

    cols = []
    for i in range(PAIRS):
        t = sc[i]
        for j in range(OWN // 8):
            cols.append(jnp.broadcast_to(t[:, 32 * j:32 * j + 1], (8, 128)))
    scale_row = jnp.concatenate(cols, 0).T[0:1, :]

    @each(LINE_FAR)
    def _(i):
        t = (z + i) & 15
        rcopy(ks, piece(kf, t), za_s.at[0], za_r.at[t], sib).wait_recv()

    for h in range(2):
        gs[h] = lax.dot_general(
            kf[...], nt[h * SLAB:(h + 1) * SLAB, :], ROW_DIMS, preferred_element_type=F32
        ).astype(BF)

    def g_copy(i):
        tx = (x + i) & 3
        return rcopy(
            gs.at[tx >> 1], gb.at[pl.ds(pl.multiple_of(place * STRIP, STRIP), STRIP), :], g_s.at[i], g_r.at[place],
            dev(tx, (y + (i >> 2)) & 3, z, core),
        )

    @each(PLANE_FAR)
    def _(i):
        g_copy(i).start()

    when_sent(g_copy, PLANE_FAR)

    gb[pl.ds(pl.multiple_of(place * STRIP, STRIP), STRIP), :] = gs[xhi]

    @each(PLANE_FAR)
    def _(i):
        t = ((y + (i >> 2)) & 3) * NX + ((x + i) & 3)
        rows = pl.ds(pl.multiple_of(t * STRIP, STRIP), STRIP)
        rcopy(gb.at[rows, :], gb.at[rows, :], g_s.at[0], g_r.at[t], sib).wait_recv()

    g_sum = jnp.zeros((1, SLAB), F32)
    gn_sum = jnp.zeros((1, SLAB), F32)
    for i in range(8):
        rows = slice(i * 128, (i + 1) * 128)
        g = gb[rows, :].astype(F32) * (2.0 * off_weight / ROWS) + no[rows, :].astype(F32) * d
        gw[rows, :] = g
        g_sum = g_sum + jnp.sum(g, 0, keepdims=True)
        gn_sum = gn_sum + jnp.sum(g * nn[rows, :].astype(F32), 0, keepdims=True)
    g_mean = g_sum / ROWS
    gn_mean = gn_sum / ROWS
    for i in range(8):
        rows = slice(i * 128, (i + 1) * 128)
        cb[rows, :] = (gw[rows, :] - g_mean - nn[rows, :].astype(F32) * gn_mean).astype(BF)

    factor = scale_row * (64.0 / ROWS)

    def product(block, i):
        rows = pl.ds(pl.multiple_of(block * BLOCK + i * 128, 128), 128)
        return jnp.dot(xt[rows, :], cb[...], preferred_element_type=F32) * factor

    for i in range(4):
        fs[i * 128:(i + 1) * 128, :] = product(1 - core, i)
    f_copy = rcopy(fs, fr, f_s, f_r, sib)
    f_copy.start()
    for i in range(4):
        out[i * 128:(i + 1) * 128, :] = product(core, i)
    f_copy.wait()
    out[...] += fr[...]

    for wait in sent:
        wait()


def local(first_view, second_view, weight):
    dma = pltpu.SemaphoreType.DMA
    vm = pltpu.VMEM
    return pl.pallas_call(
        kernel,
        out_shape=jax.ShapeDtypeStruct((BLOCK, SLAB), F32),
        in_specs=[pl.BlockSpec(memory_space=pl.ANY)] * 3,
        out_specs=pl.BlockSpec(memory_space=pltpu.VMEM),
        scratch_shapes=[
            vm((ROWS, PAIR), BF), vm((PAIR, ROWS), BF), vm((PAIR, SLAB), BF), vm((SLAB, PAIR), BF),
            vm((SLAB, ROWS), F32), vm((SLAB, ROWS), BF), vm((PAIRS, OWN, ROWS), BF), vm((2 * SLAB, ROWS), BF),
            vm((PAIRS, 8, 128), F32), vm((8, 128), F32), vm((SLAB, ROWS), BF), vm((128, 2 * SLAB), BF),
            vm((STRIP, ROWS), BF), vm((NZ, 16, 256), BF), vm((16, 256), BF), vm((STRIP, ROWS), BF),
            vm((2, STRIP, SLAB), BF), vm((ROWS, SLAB), BF), vm((ROWS, SLAB), BF), vm((ROWS, SLAB), BF),
            vm((ROWS, SLAB), F32), vm((ROWS, SLAB), BF), vm((BLOCK, SLAB), F32), vm((BLOCK, SLAB), F32),
            dma((2,)), dma((16,)), dma((16,)), dma((16,)), dma((16,)), dma, dma, dma((PAIRS,)), dma((PAIRS,)), dma((16,)), dma((16,)),
            dma((PAIRS,)), dma((PAIRS,)), dma, dma, dma((NZ,)), dma((NZ,)), dma((NZ,)), dma((NZ,)),
            dma((16,)), dma((16,)), dma, dma,
        ],
        compiler_params=pltpu.CompilerParams(collective_id=0, has_side_effects=True, vmem_limit_bytes=62 << 20),
        cost_estimate=pl.CostEstimate(flops=4 * 10**9, bytes_accessed=4 << 20, transcendentals=0),
    )(first_view, second_view, weight)


def solution(mesh):
    return jax.shard_map(
        local,
        mesh=mesh,
        in_specs=(P("batch", None), P("batch", None), P("batch", "feat")),
        out_specs=P("batch", "feat"),
        check_vma=False,
    )
```

```python
import functools

import jax
import jax.numpy as jnp
from jax import lax
from jax.experimental import pallas as pl
from jax.experimental.pallas import tpu as pltpu
from jax.sharding import PartitionSpec as P

MESH = pl.DeviceIdType.MESH
off_weight = 0.0051
NX, NY, NZ = 4, 4, 16
ROWS = 1024
BLOCK = 512
SLAB = 256
PAIR = 2 * BLOCK
PAIRS = 8
OWN = SLAB // PAIRS
HALF_OWN = OWN // 2
STRIP = ROWS // (NX * NY)
BF = jnp.bfloat16
F32 = jnp.float32

ROW_DIMS = (((1,), (1,)), ((), ()))


def coords():
    b = lax.axis_index("batch")
    f = lax.axis_index("feat")
    return (f & 1) * 2 + ((b >> 1) & 1), b >> 2, f >> 1, b & 1


def dev(x, y, z, core):
    return (y * 4 + (x & 1) * 2 + core, z * 2 + (x >> 1))


def each(values):
    def run(body):
        for i in values:
            body(i)

    return run


def ring(step, size):
    return min(step, size - step)


PLANE_FAR = sorted(range(1, 16), key=lambda i: -ring(i & 3, 4) - ring(i >> 2, 4))
GROUP_FAR = sorted(range(1, PAIRS), key=lambda i: -(i & 1) - ring(i >> 1, 4))
X_ORDER = [(1, 1), (3, 1), (1, 0), (3, 0), (2, 1), (2, 0), (0, 1)]
WHOLE = [(0, 1)]
LINE_FAR = sorted(range(NZ), key=lambda i: -ring(i, NZ))


def rcopy(src, dst, send, recv, device):
    return pltpu.make_async_remote_copy(
        src_ref=src, dst_ref=dst, send_sem=send, recv_sem=recv, device_id=device, device_id_type=MESH
    )


def kernel(
    first, second, w, out,
    xb, xt, wb, wt, pt, ptb, rsb, nt, sc, scb, noth, kl, kp, zb, ks, kf, gs, gb, nn, no, gw, cb, fs, fr,
    loc, x_s, x_r, q_s, q_r, w_s, w_r, rs_s, rs_r, ag_s, ag_r, sc_s, sc_r, n_s, n_r, zr_s, zr_r, za_s, za_r, g_s, g_r, f_s, f_r,
):
    x, y, z, core = coords()
    xlo, xhi = x & 1, x >> 1
    pair = y * 2 + xlo
    place = y * NX + x
    sib = dev(x, y, z, 1 - core)
    sent = []

    def when_sent(copy, values):
        def wait():
            for i in values:
                copy(i).wait_send()

        sent.append(wait)

    barrier = pltpu.get_barrier_semaphore()
    pl.semaphore_signal(barrier, 1, device_id=sib, device_id_type=MESH)

    @each(PLANE_FAR)
    def _(i):
        for c in range(2):
            pl.semaphore_signal(
                barrier, 1, device_id=dev((x + i) & 3, (y + (i >> 2)) & 3, z, c), device_id_type=MESH
            )

    @each(LINE_FAR[:-1])
    def _(i):
        for c in range(2):
            pl.semaphore_signal(barrier, 1, device_id=dev(x, y, (z + i) & 15, c), device_id_type=MESH)

    pl.semaphore_wait(barrier, 1 + 2 * (NX * NY - 1) + 2 * (NZ - 1))

    mine = pair * 2 + core

    half = z & 1

    def half_cols(h):
        return pl.ds(pl.multiple_of(h * BLOCK, BLOCK), BLOCK)

    def batch_rows(b):
        return pl.ds(pl.multiple_of(b * 64, 64), 64)

    def x_copy(view, dy, dlo):
        ty = (y + dy) & 3
        tlo = xlo ^ dlo
        tx = x if dlo == 0 else (x ^ 1 if view == 0 else 3 - x)
        src = (first, second)[view]
        if (dy, dlo) in WHOLE:
            col = pl.ds(pl.multiple_of((ty * 2 + tlo) * PAIR, PAIR), PAIR)
            there = xb.at[batch_rows(mine), :]
        else:
            col = pl.ds(pl.multiple_of((ty * 2 + tlo) * PAIR + half * BLOCK, BLOCK), BLOCK)
            there = xb.at[batch_rows(mine), half_cols(half)]
        return rcopy(
            src.at[:, col],
            there,
            x_s.at[(dy * 2 + dlo) * 2 + view],
            x_r.at[mine],
            dev(tx, ty, z, view),
        )

    def sib_copy(view):
        src = (first, second)[view]
        return rcopy(
            src.at[:, pl.ds(pl.multiple_of(pair * PAIR, PAIR), PAIR)],
            xb.at[batch_rows(mine), :],
            x_s.at[0],
            x_r.at[mine],
            sib,
        )

    def own_copy(view):
        src = (first, second)[view]
        return pltpu.make_async_copy(
            src.at[:, pl.ds(pl.multiple_of(pair * PAIR, PAIR), PAIR)],
            xb.at[batch_rows(mine), :],
            loc.at[0],
        )

    for dy, dlo in X_ORDER:
        for view in range(2):
            x_copy(view, dy, dlo).start()
    for view in range(2):
        @pl.when(core == view)
        def _():
            own_copy(view).start()

        @pl.when(core != view)
        def _():
            sib_copy(view).start()

    def x_sent():
        for dy, dlo in X_ORDER:
            for view in range(2):
                x_copy(view, dy, dlo).wait_send()
        for view in range(2):
            @pl.when(core != view)
            def _():
                sib_copy(view).wait_send()

    sent.append(x_sent)

    w_place = wb.at[pl.ds(pl.multiple_of(core * BLOCK, BLOCK), BLOCK), :]
    w_copy = rcopy(w, w_place, w_s, w_r, sib)
    w_copy.start()
    w_own = pltpu.make_async_copy(w, w_place, loc.at[1])
    w_own.start()
    w_own.wait()
    w_copy.wait()
    for i in range(PAIR // SLAB):
        wt[:, i * SLAB:(i + 1) * SLAB] = wb[i * SLAB:(i + 1) * SLAB, :].T
    def chunk_of(dy, dlo):
        return ((y + dy) & 3) * 2 + (xlo ^ dlo)

    def relay(dy, dlo, c):
        b = chunk_of(dy, dlo) * 2 + c
        place_there = xb.at[batch_rows(b), half_cols(half)]
        return rcopy(
            place_there, place_there, q_s.at[(dy * 2 + dlo) * 2 + c], q_r.at[b],
            dev(x, y, (z + (1 if c == 0 else 15)) & 15, core),
        )

    def product_of(chunk, h, add):
        rows = pl.ds(pl.multiple_of(chunk * 128, 128), 128)
        xs = xb[rows, half_cols(h)]
        part = lax.dot_general(wt[:, half_cols(h)], xs, ROW_DIMS, preferred_element_type=F32)
        pt[:, rows] = pt[:, rows] + part if add else part
        xt[half_cols(h), rows] = xs.T

    for dy, dlo in X_ORDER:
        for c in range(2):
            b = chunk_of(dy, dlo) * 2 + c
            if (dy, dlo) in WHOLE:
                got = xb.at[batch_rows(b), :]
                rcopy(got, got, x_s.at[0], x_r.at[b], sib).wait_recv()
            else:
                got = xb.at[batch_rows(b), half_cols(half)]
                rcopy(got, got, x_s.at[0], x_r.at[b], sib).wait_recv()
                relay(dy, dlo, c).start()
        product_of(chunk_of(dy, dlo), half, False)
        if (dy, dlo) in WHOLE:
            product_of(chunk_of(dy, dlo), 1 - half, True)

    relayed = [offset for offset in X_ORDER if offset not in WHOLE]

    def relay_sent():
        for dy, dlo in relayed:
            for c in range(2):
                relay(dy, dlo, c).wait_send()

    sent.append(relay_sent)

    for view in range(2):
        @pl.when(core == view)
        def _():
            own_copy(view).wait()
    got = xb.at[batch_rows(pair * 2 + 1 - core), :]
    rcopy(got, got, x_s.at[0], x_r.at[pair * 2 + 1 - core], sib).wait_recv()
    product_of(pair, half, False)
    product_of(pair, 1 - half, True)

    for dy, dlo in relayed:
        for c in range(2):
            b = chunk_of(dy, dlo) * 2 + c
            got = xb.at[batch_rows(b), half_cols(1 - half)]
            rcopy(got, got, q_s.at[0], q_r.at[b], sib).wait_recv()
        product_of(chunk_of(dy, dlo), 1 - half, True)

    def rs_copy(k):
        i, part = k & 7, k >> 3
        ty = (y + (i >> 1)) & 3
        tlo = xlo ^ (i & 1)
        rows = pl.ds(pl.multiple_of((ty * 2 + tlo) * OWN + part * HALF_OWN, HALF_OWN), HALF_OWN)
        return rcopy(
            ptb.at[rows, :], rsb.at[pair, part], rs_s.at[k], rs_r.at[part * PAIRS + pair],
            dev(xhi * 2 + tlo, ty, z, core),
        )

    def own_rows(part):
        return pl.ds(pl.multiple_of(xhi * SLAB + pair * OWN + part * HALF_OWN, HALF_OWN), HALF_OWN)

    def ag_copy(k):
        i, part = k & 15, k >> 4
        return rcopy(
            nt.at[own_rows(part), :], nt.at[own_rows(part), :], ag_s.at[k], ag_r.at[part * 16 + place],
            dev((x + i) & 3, (y + (i >> 2)) & 3, z, core),
        )

    for part in range(2):
        for i in range(PAIRS):
            rows = slice(i * OWN + part * HALF_OWN, i * OWN + (part + 1) * HALF_OWN)
            values = pt[rows, :]
            ptb[rows, :] = (values - jnp.mean(values, 1, keepdims=True)).astype(BF)
        for i in GROUP_FAR:
            rs_copy(part * PAIRS + i).start()
        when_sent(rs_copy, [part * PAIRS + i for i in GROUP_FAR])

    scales = []
    for part in range(2):
        rsb[pair, part] = ptb[pl.ds(pl.multiple_of(pair * OWN + part * HALF_OWN, HALF_OWN), HALF_OWN), :]
        for i in GROUP_FAR:
            other = (pair + i) & 7
            got = rsb.at[other, part]
            rcopy(got, got, rs_s.at[0], rs_r.at[part * PAIRS + other], sib).wait_recv()
        total = rsb[0, part].astype(F32)
        for i in range(1, PAIRS):
            total = total + rsb[i, part].astype(F32)
        mean = jnp.sum(total, 1, keepdims=True) / ROWS
        spread = jnp.sum(total * total, 1, keepdims=True) / ROWS - mean * mean
        scales.append(lax.rsqrt(spread + 1e-05))
        nt[own_rows(part), :] = ((total - mean) * scales[part]).astype(BF)
        for i in PLANE_FAR:
            ag_copy(part * 16 + i).start()
        when_sent(ag_copy, [part * 16 + i for i in PLANE_FAR])
    scale = jnp.concatenate(scales, 0)
    lane = lax.broadcasted_iota(jnp.int32, (8, 128), 1)
    wide = jnp.broadcast_to(scale, (OWN, 128))
    tile = wide[0:8]
    for i in range(1, OWN // 8):
        tile = jnp.where(lane >= 32 * i, wide[8 * i:8 * i + 8], tile)
    sc[pair] = tile

    def sc_copy(i):
        return rcopy(
            sc.at[pair], sc.at[pair], sc_s.at[i], sc_r.at[pair],
            dev(xhi * 2 + xlo ^ (i & 1), (y + (i >> 1)) & 3, z, core),
        )

    @each(GROUP_FAR)
    def _(i):
        sc_copy(i).start()

    when_sent(sc_copy, GROUP_FAR)

    for part in range(2):
        for i in PLANE_FAR:
            sx, sy = (x + i) & 3, (y + (i >> 2)) & 3
            first_row = (sx >> 1) * SLAB + (sy * 2 + (sx & 1)) * OWN + part * HALF_OWN
            got = nt.at[pl.ds(pl.multiple_of(first_row, HALF_OWN), HALF_OWN), :]
            rcopy(got, got, ag_s.at[0], ag_r.at[part * 16 + sy * NX + sx], sib).wait_recv()

    @each(GROUP_FAR)
    def _(i):
        other = (pair + i) & 7
        rcopy(sc.at[other], sc.at[other], sc_s.at[0], sc_r.at[other], sib).wait_recv()

    kl[...] = nt[:, pl.ds(pl.multiple_of((place >> 1) * 128, 128), 128)].T
    strip = kl[pl.ds(pl.multiple_of((place & 1) * STRIP, STRIP), STRIP), :]
    for i in range(4):
        kp[:, i * 256:(i + 1) * 256] = jnp.dot(
            strip, nt[:, i * 256:(i + 1) * 256], preferred_element_type=F32
        ).astype(BF)

    def piece(ref, t):
        return ref.at[pl.ds(pl.multiple_of((t >> 2) * 16, 16), 16), pl.ds(pl.multiple_of((t & 3) * 256, 256), 256)]

    def zr_copy(i):
        t = (z + i) & 15
        return rcopy(piece(kp, t), zb.at[z], zr_s.at[i], zr_r.at[z], dev(x, y, t, core))

    @each(LINE_FAR[:-1])
    def _(i):
        zr_copy(i).start()

    when_sent(zr_copy, LINE_FAR[:-1])

    slab_rows = pl.ds(pl.multiple_of(xhi * SLAB, SLAB), SLAB)
    n_copy = rcopy(nt.at[slab_rows, :], noth, n_s, n_r, sib)
    n_copy.start()

    zb[z] = kp[
        pl.ds(pl.multiple_of((z >> 2) * 16, 16), 16), pl.ds(pl.multiple_of((z & 3) * 256, 256), 256)
    ]

    @each(LINE_FAR[:-1])
    def _(i):
        t = (z + i) & 15
        rcopy(zb.at[t], zb.at[t], zr_s.at[0], zr_r.at[t], sib).wait_recv()

    n_copy.wait()
    acc = zb[0].astype(F32)
    for i in range(1, NZ):
        acc = acc + zb[i].astype(F32)
    ks[...] = acc.astype(BF)

    def za_copy(i):
        return rcopy(ks, piece(kf, z), za_s.at[i], za_r.at[z], dev(x, y, (z + i) & 15, 1 - core))

    @each(LINE_FAR)
    def _(i):
        za_copy(i).start()

    when_sent(za_copy, LINE_FAR)

    for i in range(8):
        rows = slice(i * 128, (i + 1) * 128)
        nn[rows, :] = nt[slab_rows, rows].T
        no[rows, :] = noth[:, rows].T
    diag = jnp.zeros((1, SLAB), F32)
    for i in range(8):
        rows = slice(i * 128, (i + 1) * 128)
        diag = diag + jnp.sum(nn[rows, :].astype(F32) * no[rows, :].astype(F32), 0, keepdims=True)
    diag = diag / ROWS
    d = -2.0 * (1.0 - diag) - 2.0 * off_weight * diag

    cols = []
    for i in range(PAIRS):
        t = sc[i]
        for j in range(OWN // 8):
            cols.append(jnp.broadcast_to(t[:, 32 * j:32 * j + 1], (8, 128)))
    scale_row = jnp.concatenate(cols, 0).T[0:1, :]

    @each(LINE_FAR)
    def _(i):
        t = (z + i) & 15
        rcopy(ks, piece(kf, t), za_s.at[0], za_r.at[t], sib).wait_recv()

    for h in range(2):
        gs[h] = lax.dot_general(
            kf[...], nt[h * SLAB:(h + 1) * SLAB, :], ROW_DIMS, preferred_element_type=F32
        ).astype(BF)

    def g_copy(i):
        tx = (x + i) & 3
        return rcopy(
            gs.at[tx >> 1], gb.at[pl.ds(pl.multiple_of(place * STRIP, STRIP), STRIP), :], g_s.at[i], g_r.at[place],
            dev(tx, (y + (i >> 2)) & 3, z, core),
        )

    @each(PLANE_FAR)
    def _(i):
        g_copy(i).start()

    when_sent(g_copy, PLANE_FAR)

    gb[pl.ds(pl.multiple_of(place * STRIP, STRIP), STRIP), :] = gs[xhi]

    @each(PLANE_FAR)
    def _(i):
        t = ((y + (i >> 2)) & 3) * NX + ((x + i) & 3)
        rows = pl.ds(pl.multiple_of(t * STRIP, STRIP), STRIP)
        rcopy(gb.at[rows, :], gb.at[rows, :], g_s.at[0], g_r.at[t], sib).wait_recv()

    g_sum = jnp.zeros((1, SLAB), F32)
    gn_sum = jnp.zeros((1, SLAB), F32)
    for i in range(8):
        rows = slice(i * 128, (i + 1) * 128)
        g = gb[rows, :].astype(F32) * (2.0 * off_weight / ROWS) + no[rows, :].astype(F32) * d
        gw[rows, :] = g
        g_sum = g_sum + jnp.sum(g, 0, keepdims=True)
        gn_sum = gn_sum + jnp.sum(g * nn[rows, :].astype(F32), 0, keepdims=True)
    g_mean = g_sum / ROWS
    gn_mean = gn_sum / ROWS
    for i in range(8):
        rows = slice(i * 128, (i + 1) * 128)
        cb[rows, :] = (gw[rows, :] - g_mean - nn[rows, :].astype(F32) * gn_mean).astype(BF)

    factor = scale_row * (64.0 / ROWS)

    def product(block, i):
        rows = pl.ds(pl.multiple_of(block * BLOCK + i * 128, 128), 128)
        return jnp.dot(xt[rows, :], cb[...], preferred_element_type=F32) * factor

    for i in range(4):
        fs[i * 128:(i + 1) * 128, :] = product(1 - core, i)
    f_copy = rcopy(fs, fr, f_s, f_r, sib)
    f_copy.start()
    for i in range(4):
        out[i * 128:(i + 1) * 128, :] = product(core, i)
    f_copy.wait()
    out[...] += fr[...]

    for wait in sent:
        wait()


def local(first_view, second_view, weight):
    dma = pltpu.SemaphoreType.DMA
    vm = pltpu.VMEM
    return pl.pallas_call(
        kernel,
        out_shape=jax.ShapeDtypeStruct((BLOCK, SLAB), F32),
        in_specs=[pl.BlockSpec(memory_space=pl.ANY)] * 3,
        out_specs=pl.BlockSpec(memory_space=pltpu.VMEM),
        scratch_shapes=[
            vm((ROWS, PAIR), BF), vm((PAIR, ROWS), BF), vm((PAIR, SLAB), BF), vm((SLAB, PAIR), BF),
            vm((SLAB, ROWS), F32), vm((SLAB, ROWS), BF), vm((PAIRS, 2, HALF_OWN, ROWS), BF), vm((2 * SLAB, ROWS), BF),
            vm((PAIRS, 8, 128), F32), vm((8, 128), F32), vm((SLAB, ROWS), BF), vm((128, 2 * SLAB), BF),
            vm((STRIP, ROWS), BF), vm((NZ, 16, 256), BF), vm((16, 256), BF), vm((STRIP, ROWS), BF),
            vm((2, STRIP, SLAB), BF), vm((ROWS, SLAB), BF), vm((ROWS, SLAB), BF), vm((ROWS, SLAB), BF),
            vm((ROWS, SLAB), F32), vm((ROWS, SLAB), BF), vm((BLOCK, SLAB), F32), vm((BLOCK, SLAB), F32),
            dma((2,)), dma((16,)), dma((16,)), dma((16,)), dma((16,)), dma, dma, dma((16,)), dma((16,)), dma((32,)), dma((32,)),
            dma((PAIRS,)), dma((PAIRS,)), dma, dma, dma((NZ,)), dma((NZ,)), dma((NZ,)), dma((NZ,)),
            dma((16,)), dma((16,)), dma, dma,
        ],
        compiler_params=pltpu.CompilerParams(collective_id=0, has_side_effects=True, vmem_limit_bytes=62 << 20),
        cost_estimate=pl.CostEstimate(flops=4 * 10**9, bytes_accessed=4 << 20, transcendentals=0),
    )(first_view, second_view, weight)


def solution(mesh):
    return jax.shard_map(
        local,
        mesh=mesh,
        in_specs=(P("batch", None), P("batch", None), P("batch", "feat")),
        out_specs=P("batch", "feat"),
        check_vma=False,
    )
```

```python
import functools

import jax
import jax.numpy as jnp
from jax import lax
from jax.experimental import pallas as pl
from jax.experimental.pallas import tpu as pltpu
from jax.sharding import PartitionSpec as P

MESH = pl.DeviceIdType.MESH
off_weight = 0.0051
NX, NY, NZ = 4, 4, 16
ROWS = 1024
BLOCK = 512
SLAB = 256
PAIR = 2 * BLOCK
PAIRS = 8
OWN = SLAB // PAIRS
HALF_OWN = OWN // 2
HALF_SLAB = SLAB // 2
STRIP = ROWS // (NX * NY)
BF = jnp.bfloat16
F32 = jnp.float32

ROW_DIMS = (((1,), (1,)), ((), ()))


def coords():
    b = lax.axis_index("batch")
    f = lax.axis_index("feat")
    return (f & 1) * 2 + ((b >> 1) & 1), b >> 2, f >> 1, b & 1


def dev(x, y, z, core):
    return (y * 4 + (x & 1) * 2 + core, z * 2 + (x >> 1))


def each(values):
    def run(body):
        for i in values:
            body(i)

    return run


def ring(step, size):
    return min(step, size - step)


PLANE_FAR = sorted(range(1, 16), key=lambda i: -ring(i & 3, 4) - ring(i >> 2, 4))
GROUP_FAR = sorted(range(1, PAIRS), key=lambda i: -(i & 1) - ring(i >> 1, 4))
X_ORDER = [(1, 1), (3, 1), (1, 0), (3, 0), (2, 1), (2, 0), (0, 1)]
WHOLE = [(0, 1)]
LINE_FAR = sorted(range(NZ), key=lambda i: -ring(i, NZ))


def rcopy(src, dst, send, recv, device):
    return pltpu.make_async_remote_copy(
        src_ref=src, dst_ref=dst, send_sem=send, recv_sem=recv, device_id=device, device_id_type=MESH
    )


def kernel(
    first, second, w, out,
    xb, xt, wb, wt, pt, ptb, rsb, nt, sc, scb, noth, kl, kp, zb, ks, kf, gs, gb, nn, no, gw, cb, fs, fr,
    loc, x_s, x_r, q_s, q_r, w_s, w_r, rs_s, rs_r, ag_s, ag_r, sc_s, sc_r, n_s, n_r, zr_s, zr_r, za_s, za_r, g_s, g_r, f_s, f_r,
    sw_s, sw_r, ns_s, ns_r, ns, ka,
):
    x, y, z, core = coords()
    xlo, xhi = x & 1, x >> 1
    pair = y * 2 + xlo
    place = y * NX + x
    sib = dev(x, y, z, 1 - core)
    sent = []

    def when_sent(copy, values):
        def wait():
            for i in values:
                copy(i).wait_send()

        sent.append(wait)

    barrier = pltpu.get_barrier_semaphore()
    pl.semaphore_signal(barrier, 1, device_id=sib, device_id_type=MESH)

    @each(PLANE_FAR)
    def _(i):
        for c in range(2):
            pl.semaphore_signal(
                barrier, 1, device_id=dev((x + i) & 3, (y + (i >> 2)) & 3, z, c), device_id_type=MESH
            )

    @each(LINE_FAR[:-1])
    def _(i):
        for c in range(2):
            pl.semaphore_signal(barrier, 1, device_id=dev(x ^ c, y, (z + i) & 15, core), device_id_type=MESH)

    pl.semaphore_wait(barrier, 1 + 2 * (NX * NY - 1) + 2 * (NZ - 1))

    mine = pair * 2 + core

    half = z & 1

    def half_cols(h):
        return pl.ds(pl.multiple_of(h * BLOCK, BLOCK), BLOCK)

    def batch_rows(b):
        return pl.ds(pl.multiple_of(b * 64, 64), 64)

    def x_copy(view, dy, dlo):
        ty = (y + dy) & 3
        tlo = xlo ^ dlo
        tx = x if dlo == 0 else (x ^ 1 if view == 0 else 3 - x)
        src = (first, second)[view]
        if (dy, dlo) in WHOLE:
            col = pl.ds(pl.multiple_of((ty * 2 + tlo) * PAIR, PAIR), PAIR)
            there = xb.at[batch_rows(mine), :]
        else:
            col = pl.ds(pl.multiple_of((ty * 2 + tlo) * PAIR + half * BLOCK, BLOCK), BLOCK)
            there = xb.at[batch_rows(mine), half_cols(half)]
        return rcopy(
            src.at[:, col],
            there,
            x_s.at[(dy * 2 + dlo) * 2 + view],
            x_r.at[mine],
            dev(tx, ty, z, view),
        )

    def sib_copy(view):
        src = (first, second)[view]
        return rcopy(
            src.at[:, pl.ds(pl.multiple_of(pair * PAIR, PAIR), PAIR)],
            xb.at[batch_rows(mine), :],
            x_s.at[0],
            x_r.at[mine],
            sib,
        )

    def own_copy(view):
        src = (first, second)[view]
        return pltpu.make_async_copy(
            src.at[:, pl.ds(pl.multiple_of(pair * PAIR, PAIR), PAIR)],
            xb.at[batch_rows(mine), :],
            loc.at[0],
        )

    for dy, dlo in X_ORDER:
        for view in range(2):
            x_copy(view, dy, dlo).start()
    for view in range(2):
        @pl.when(core == view)
        def _():
            own_copy(view).start()

        @pl.when(core != view)
        def _():
            sib_copy(view).start()

    def x_sent():
        for dy, dlo in X_ORDER:
            for view in range(2):
                x_copy(view, dy, dlo).wait_send()
        for view in range(2):
            @pl.when(core != view)
            def _():
                sib_copy(view).wait_send()

    sent.append(x_sent)

    w_place = wb.at[pl.ds(pl.multiple_of(core * BLOCK, BLOCK), BLOCK), :]
    w_copy = rcopy(w, w_place, w_s, w_r, sib)
    w_copy.start()
    w_own = pltpu.make_async_copy(w, w_place, loc.at[1])
    w_own.start()
    w_own.wait()
    w_copy.wait()
    for i in range(PAIR // SLAB):
        wt[:, i * SLAB:(i + 1) * SLAB] = wb[i * SLAB:(i + 1) * SLAB, :].T
    def chunk_of(dy, dlo):
        return ((y + dy) & 3) * 2 + (xlo ^ dlo)

    def relay(dy, dlo, c):
        b = chunk_of(dy, dlo) * 2 + c
        place_there = xb.at[batch_rows(b), half_cols(half)]
        return rcopy(
            place_there, place_there, q_s.at[(dy * 2 + dlo) * 2 + c], q_r.at[b],
            dev(x, y, (z + (1 if c == 0 else 15)) & 15, core),
        )

    def product_of(chunk, h, add):
        rows = pl.ds(pl.multiple_of(chunk * 128, 128), 128)
        xs = xb[rows, half_cols(h)]
        part = lax.dot_general(wt[:, half_cols(h)], xs, ROW_DIMS, preferred_element_type=F32)
        pt[:, rows] = pt[:, rows] + part if add else part
        xt[half_cols(h), rows] = xs.T

    for dy, dlo in X_ORDER:
        for c in range(2):
            b = chunk_of(dy, dlo) * 2 + c
            if (dy, dlo) in WHOLE:
                got = xb.at[batch_rows(b), :]
                rcopy(got, got, x_s.at[0], x_r.at[b], sib).wait_recv()
            else:
                got = xb.at[batch_rows(b), half_cols(half)]
                rcopy(got, got, x_s.at[0], x_r.at[b], sib).wait_recv()
                relay(dy, dlo, c).start()
        product_of(chunk_of(dy, dlo), half, False)
        if (dy, dlo) in WHOLE:
            product_of(chunk_of(dy, dlo), 1 - half, True)

    relayed = [offset for offset in X_ORDER if offset not in WHOLE]

    def relay_sent():
        for dy, dlo in relayed:
            for c in range(2):
                relay(dy, dlo, c).wait_send()

    sent.append(relay_sent)

    for view in range(2):
        @pl.when(core == view)
        def _():
            own_copy(view).wait()
    got = xb.at[batch_rows(pair * 2 + 1 - core), :]
    rcopy(got, got, x_s.at[0], x_r.at[pair * 2 + 1 - core], sib).wait_recv()
    product_of(pair, half, False)
    product_of(pair, 1 - half, True)

    for dy, dlo in relayed:
        for c in range(2):
            b = chunk_of(dy, dlo) * 2 + c
            got = xb.at[batch_rows(b), half_cols(1 - half)]
            rcopy(got, got, q_s.at[0], q_r.at[b], sib).wait_recv()
        product_of(chunk_of(dy, dlo), 1 - half, True)

    def part_rows(part, p):
        return pl.ds(pl.multiple_of(part * HALF_SLAB + p * HALF_OWN, HALF_OWN), HALF_OWN)

    def rs_copy(k):
        i, part = k & 7, k >> 3
        ty = (y + (i >> 1)) & 3
        tlo = xlo ^ (i & 1)
        return rcopy(
            ptb.at[part_rows(part, ty * 2 + tlo), :], rsb.at[pair, part], rs_s.at[k], rs_r.at[part * PAIRS + pair],
            dev(xhi * 2 + tlo, ty, z, core),
        )

    def plane_rows(h, part, p):
        return pl.ds(pl.multiple_of(h * SLAB + part * HALF_SLAB + p * HALF_OWN, HALF_OWN), HALF_OWN)

    def ag_copy(k):
        part, h, dy = k >> 3, (k >> 2) & 1, k & 3
        return rcopy(
            ns.at[part_rows(part, pair), :], nt.at[plane_rows(xhi, part, pair), :], ag_s.at[k],
            ag_r.at[part * PAIRS + pair], dev(core + 2 * h, (y + dy) & 3, z, xhi),
        )

    alone = jnp.logical_and(core == xlo, core == xhi)

    def ag_far(part):
        return [part * 8 + h * 4 + dy for dy in (2, 1, 3, 0) for h in range(2)]

    def unless_mine(k, do):
        if k & 3 == 0:
            h = (k >> 2) & 1

            @pl.when(jnp.logical_not(jnp.logical_and(alone, xhi == h)))
            def _():
                do(ag_copy(k))
        else:
            do(ag_copy(k))

    def ag_sent():
        for k in range(16):
            unless_mine(k, lambda copy: copy.wait_send())

    sent.append(ag_sent)

    for part in range(2):
        for i in range(PAIRS):
            rows = slice(part * HALF_SLAB + i * HALF_OWN, part * HALF_SLAB + (i + 1) * HALF_OWN)
            values = pt[rows, :]
            ptb[rows, :] = (values - jnp.mean(values, 1, keepdims=True)).astype(BF)
        for i in GROUP_FAR:
            rs_copy(part * PAIRS + i).start()
        when_sent(rs_copy, [part * PAIRS + i for i in GROUP_FAR])

    scales = []
    for part in range(2):
        rsb[pair, part] = ptb[part_rows(part, pair), :]
        for i in GROUP_FAR:
            other = (pair + i) & 7
            got = rsb.at[other, part]
            rcopy(got, got, rs_s.at[0], rs_r.at[part * PAIRS + other], sib).wait_recv()
        total = rsb[0, part].astype(F32)
        for i in range(1, PAIRS):
            total = total + rsb[i, part].astype(F32)
        mean = jnp.sum(total, 1, keepdims=True) / ROWS
        spread = jnp.sum(total * total, 1, keepdims=True) / ROWS - mean * mean
        scales.append(lax.rsqrt(spread + 1e-05))
        normed = ((total - mean) * scales[part]).astype(BF)
        ns[part_rows(part, pair), :] = normed

        @pl.when(alone)
        def _():
            nt[plane_rows(xhi, part, pair), :] = normed

        for k in ag_far(part):
            unless_mine(k, lambda copy: copy.start())
    scale = jnp.concatenate(scales, 0)
    lane = lax.broadcasted_iota(jnp.int32, (8, 128), 1)
    wide = jnp.broadcast_to(scale, (OWN, 128))
    tile = wide[0:8]
    for i in range(1, OWN // 8):
        tile = jnp.where(lane >= 32 * i, wide[8 * i:8 * i + 8], tile)
    sc[pair] = tile

    def sc_copy(i):
        return rcopy(
            sc.at[pair], sc.at[pair], sc_s.at[i], sc_r.at[pair],
            dev(xhi * 2 + xlo ^ (i & 1), (y + (i >> 1)) & 3, z, core),
        )

    @each(GROUP_FAR)
    def _(i):
        sc_copy(i).start()

    when_sent(sc_copy, GROUP_FAR)

    strip_place = (y * 2 + xhi) * 2 + core
    lanes = pl.ds(pl.multiple_of((strip_place >> 1) * 128, 128), 128)

    def swap(part):
        rows = pl.ds(pl.multiple_of(core * SLAB + part * HALF_SLAB, HALF_SLAB), HALF_SLAB)
        return rcopy(nt.at[rows, :], nt.at[rows, :], sw_s.at[part], sw_r.at[part], sib)

    for part in range(2):
        for i in GROUP_FAR + [0]:
            other = (pair + i) & 7
            got = nt.at[plane_rows(core, part, other), :]

            def arrived():
                rcopy(got, got, ag_s.at[0], ag_r.at[part * PAIRS + other], sib).wait_recv()

            if i == 0:
                pl.when(jnp.logical_not(alone))(arrived)
            else:
                arrived()
        swap(part).start()
        swap(part).wait()
        for h in range(2):
            columns = slice(h * SLAB + part * HALF_SLAB, h * SLAB + (part + 1) * HALF_SLAB)
            kl[h] = nt[columns, lanes].T
            strip = kl[h, pl.ds(pl.multiple_of(core * STRIP, STRIP), STRIP), :]
            for i in range(4):
                cols = slice(i * 256, (i + 1) * 256)
                term = jnp.dot(strip, nt[columns, cols], preferred_element_type=F32)
                if part == 0 and h == 0:
                    ka[:, cols] = term
                elif part == 1 and h == 1:
                    kp[:, cols] = (ka[:, cols] + term).astype(BF)
                else:
                    ka[:, cols] += term

    @each(GROUP_FAR)
    def _(i):
        other = (pair + i) & 7
        rcopy(sc.at[other], sc.at[other], sc_s.at[0], sc_r.at[other], sib).wait_recv()

    def piece(ref, t):
        return ref.at[pl.ds(pl.multiple_of((t >> 2) * 16, 16), 16), pl.ds(pl.multiple_of((t & 3) * 256, 256), 256)]

    def zr_copy(i):
        t = (z + i) & 15
        return rcopy(piece(kp, t), zb.at[z], zr_s.at[i], zr_r.at[z], dev(x, y, t, core))

    @each(LINE_FAR[:-1])
    def _(i):
        zr_copy(i).start()

    when_sent(zr_copy, LINE_FAR[:-1])

    def ns_copy(k):
        i, part = k & 7, k >> 3
        rows = part_rows(part, pair)
        return rcopy(
            ns.at[rows, :], ns.at[rows, :], ns_s.at[k], ns_r.at[part * PAIRS + pair],
            dev(xhi * 2 + (xlo ^ (i & 1)), (y + (i >> 1)) & 3, z, core),
        )

    ns_all = [part * PAIRS + i for i in GROUP_FAR for part in range(2)]
    for k in ns_all:
        ns_copy(k).start()
    when_sent(ns_copy, ns_all)

    zb[z] = kp[
        pl.ds(pl.multiple_of((z >> 2) * 16, 16), 16), pl.ds(pl.multiple_of((z & 3) * 256, 256), 256)
    ]

    @each(LINE_FAR[:-1])
    def _(i):
        t = (z + i) & 15
        rcopy(zb.at[t], zb.at[t], zr_s.at[0], zr_r.at[t], sib).wait_recv()

    acc = zb[0].astype(F32)
    for i in range(1, NZ):
        acc = acc + zb[i].astype(F32)
    ks[...] = acc.astype(BF)

    def za_copy(i):
        return rcopy(ks, piece(kf, z), za_s.at[i], za_r.at[z], dev(x ^ 1, y, (z + i) & 15, core))

    @each(LINE_FAR)
    def _(i):
        za_copy(i).start()

    when_sent(za_copy, LINE_FAR)

    for k in ns_all:
        i, part = k & 7, k >> 3
        other = (pair + i) & 7
        got = ns.at[part_rows(part, other), :]
        rcopy(got, got, ns_s.at[0], ns_r.at[part * PAIRS + other], sib).wait_recv()
    n_copy = rcopy(ns, noth, n_s, n_r, sib)
    n_copy.start()
    for i in range(8):
        rows = slice(i * 128, (i + 1) * 128)
        nn[rows, :] = ns[:, rows].T
    n_copy.wait()
    for i in range(8):
        rows = slice(i * 128, (i + 1) * 128)
        no[rows, :] = noth[:, rows].T
    diag = jnp.zeros((1, SLAB), F32)
    for i in range(8):
        rows = slice(i * 128, (i + 1) * 128)
        diag = diag + jnp.sum(nn[rows, :].astype(F32) * no[rows, :].astype(F32), 0, keepdims=True)
    diag = diag / ROWS
    d = -2.0 * (1.0 - diag) - 2.0 * off_weight * diag

    cols = []
    for part in range(2):
        for i in range(PAIRS):
            t = sc[i]
            for j in (2 * part, 2 * part + 1):
                cols.append(jnp.broadcast_to(t[:, 32 * j:32 * j + 1], (8, 128)))
    scale_row = jnp.concatenate(cols, 0).T[0:1, :]

    for i in LINE_FAR:
        t = (z + i) & 15
        rcopy(ks, piece(kf, t), za_s.at[0], za_r.at[t], sib).wait_recv()

    def g_rows(s):
        return pl.ds(pl.multiple_of(s * STRIP, STRIP), STRIP)

    def g_copy(i):
        tx = (x + i) & 3
        return rcopy(
            gs.at[tx >> 1], gb.at[g_rows(strip_place), :], g_s.at[i], g_r.at[strip_place],
            dev(tx, (y + (i >> 2)) & 3, z, xlo),
        )

    for h in range(2):
        gs[h] = lax.dot_general(
            kf[...], nt[h * SLAB:(h + 1) * SLAB, :], ROW_DIMS, preferred_element_type=F32
        ).astype(BF)
    for i in PLANE_FAR:
        g_copy(i).start()

    @pl.when(core == xlo)
    def _():
        gb[g_rows(strip_place), :] = gs[xhi]

    @pl.when(core != xlo)
    def _():
        g_copy(0).start()

    def g_sent():
        for i in PLANE_FAR:
            g_copy(i).wait_send()

        @pl.when(core != xlo)
        def _():
            g_copy(0).wait_send()

    sent.append(g_sent)

    for s in range(16):
        def arrived():
            got = gb.at[g_rows(s), :]
            rcopy(got, got, g_s.at[0], g_r.at[s], sib).wait_recv()

        pl.when(jnp.logical_or(core != xlo, strip_place != s))(arrived)

    g_sum = jnp.zeros((1, SLAB), F32)
    gn_sum = jnp.zeros((1, SLAB), F32)
    for i in range(8):
        rows = slice(i * 128, (i + 1) * 128)
        g = gb[rows, :].astype(F32) * (2.0 * off_weight / ROWS) + no[rows, :].astype(F32) * d
        gw[rows, :] = g
        g_sum = g_sum + jnp.sum(g, 0, keepdims=True)
        gn_sum = gn_sum + jnp.sum(g * nn[rows, :].astype(F32), 0, keepdims=True)
    g_mean = g_sum / ROWS
    gn_mean = gn_sum / ROWS
    for i in range(8):
        rows = slice(i * 128, (i + 1) * 128)
        cb[rows, :] = (gw[rows, :] - g_mean - nn[rows, :].astype(F32) * gn_mean).astype(BF)

    factor = scale_row * (64.0 / ROWS)

    def product(block, i):
        rows = pl.ds(pl.multiple_of(block * BLOCK + i * 128, 128), 128)
        return jnp.dot(xt[rows, :], cb[...], preferred_element_type=F32) * factor

    def f_copy(i):
        rows = pl.ds(i * 128, 128)
        return rcopy(fs.at[rows, :], fr.at[rows, :], f_s.at[i], f_r.at[i], sib)

    for i in range(4):
        fs[i * 128:(i + 1) * 128, :] = product(1 - core, i)
        f_copy(i).start()
    when_sent(f_copy, range(4))
    for i in range(4):
        rows = slice(i * 128, (i + 1) * 128)
        part = product(core, i)
        f_copy(i).wait_recv()
        out[rows, :] = part + fr[rows, :]

    for wait in sent:
        wait()


def local(first_view, second_view, weight):
    dma = pltpu.SemaphoreType.DMA
    vm = pltpu.VMEM
    return pl.pallas_call(
        kernel,
        out_shape=jax.ShapeDtypeStruct((BLOCK, SLAB), F32),
        in_specs=[pl.BlockSpec(memory_space=pl.ANY)] * 3,
        out_specs=pl.BlockSpec(memory_space=pltpu.VMEM),
        scratch_shapes=[
            vm((ROWS, PAIR), BF), vm((PAIR, ROWS), BF), vm((PAIR, SLAB), BF), vm((SLAB, PAIR), BF),
            vm((SLAB, ROWS), F32), vm((SLAB, ROWS), BF), vm((PAIRS, 2, HALF_OWN, ROWS), BF), vm((2 * SLAB, ROWS), BF),
            vm((PAIRS, 8, 128), F32), vm((8, 128), F32), vm((SLAB, ROWS), BF), vm((2, 128, HALF_SLAB), BF),
            vm((STRIP, ROWS), BF), vm((NZ, 16, 256), BF), vm((16, 256), BF), vm((STRIP, ROWS), BF),
            vm((2, STRIP, SLAB), BF), vm((ROWS, SLAB), BF), vm((ROWS, SLAB), BF), vm((ROWS, SLAB), BF),
            vm((ROWS, SLAB), F32), vm((ROWS, SLAB), BF), vm((BLOCK, SLAB), F32), vm((BLOCK, SLAB), F32),
            dma((2,)), dma((16,)), dma((16,)), dma((16,)), dma((16,)), dma, dma, dma((16,)), dma((16,)), dma((16,)), dma((16,)),
            dma((PAIRS,)), dma((PAIRS,)), dma, dma, dma((NZ,)), dma((NZ,)), dma((NZ,)), dma((NZ,)),
            dma((16,)), dma((16,)), dma((4,)), dma((4,)),
            dma((2,)), dma((2,)), dma((16,)), dma((16,)), vm((SLAB, ROWS), BF), vm((STRIP, ROWS), F32),
        ],
        compiler_params=pltpu.CompilerParams(collective_id=0, has_side_effects=True, vmem_limit_bytes=53 << 20),
        cost_estimate=pl.CostEstimate(flops=4 * 10**9, bytes_accessed=4 << 20, transcendentals=0),
    )(first_view, second_view, weight)


def solution(mesh):
    return jax.shard_map(
        local,
        mesh=mesh,
        in_specs=(P("batch", None), P("batch", None), P("batch", "feat")),
        out_specs=P("batch", "feat"),
        check_vma=False,
    )
```

```python
import functools

import jax
import jax.numpy as jnp
from jax import lax
from jax.experimental import pallas as pl
from jax.experimental.pallas import tpu as pltpu
from jax.sharding import PartitionSpec as P

MESH = pl.DeviceIdType.MESH
off_weight = 0.0051
NX, NY, NZ = 4, 4, 16
ROWS = 1024
BLOCK = 512
SLAB = 256
PAIR = 2 * BLOCK
PAIRS = 8
OWN = SLAB // PAIRS
HALF_OWN = OWN // 2
HALF_SLAB = SLAB // 2
STRIP = ROWS // (NX * NY)
BF = jnp.bfloat16
F32 = jnp.float32

ROW_DIMS = (((1,), (1,)), ((), ()))


def coords():
    b = lax.axis_index("batch")
    f = lax.axis_index("feat")
    return (f & 1) * 2 + ((b >> 1) & 1), b >> 2, f >> 1, b & 1


def dev(x, y, z, core):
    return (y * 4 + (x & 1) * 2 + core, z * 2 + (x >> 1))


def each(values):
    def run(body):
        for i in values:
            body(i)

    return run


def ring(step, size):
    return min(step, size - step)


PLANE_FAR = sorted(range(1, 16), key=lambda i: -ring(i & 3, 4) - ring(i >> 2, 4))
GROUP_FAR = sorted(range(1, PAIRS), key=lambda i: -(i & 1) - ring(i >> 1, 4))
X_ORDER = [(1, 1), (3, 1), (1, 0), (3, 0), (2, 1), (2, 0), (0, 1)]
WHOLE = [(0, 1)]
LINE_FAR = sorted(range(NZ), key=lambda i: -ring(i, NZ))


def rcopy(src, dst, send, recv, device):
    return pltpu.make_async_remote_copy(
        src_ref=src, dst_ref=dst, send_sem=send, recv_sem=recv, device_id=device, device_id_type=MESH
    )


def kernel(
    first, second, w, out,
    xb, xt, wb, wt, pt, ptb, rsb, nt, sc, scb, noth, kl, kp, zb, ks, kf, gs, gb, nn, no, gw, cb, fs, fr,
    loc, x_s, x_r, q_s, q_r, w_s, w_r, rs_s, rs_r, ag_s, ag_r, sc_s, sc_r, n_s, n_r, zr_s, zr_r, za_s, za_r, g_s, g_r, f_s, f_r,
    sw_s, sw_r, ns_s, ns_r, ns, ka, line_sem,
):
    x, y, z, core = coords()
    xlo, xhi = x & 1, x >> 1
    pair = y * 2 + xlo
    place = y * NX + x
    sib = dev(x, y, z, 1 - core)
    sent = []

    def when_sent(copy, values):
        def wait():
            for i in values:
                copy(i).wait_send()

        sent.append(wait)

    barrier = pltpu.get_barrier_semaphore()
    pl.semaphore_signal(barrier, 1, device_id=sib, device_id_type=MESH)

    @each(PLANE_FAR)
    def _(i):
        for c in range(2):
            pl.semaphore_signal(
                barrier, 1, device_id=dev((x + i) & 3, (y + (i >> 2)) & 3, z, c), device_id_type=MESH
            )

    for i in (1, NZ - 1):
        for c in range(2):
            pl.semaphore_signal(barrier, 1, device_id=dev(x ^ c, y, (z + i) & 15, core), device_id_type=MESH)

    pl.semaphore_wait(barrier, 1 + 2 * (NX * NY - 1) + 4)

    def tell(i):
        for step in (1 << i, NZ - (1 << i)):
            pl.semaphore_signal(line_sem.at[i], 1, device_id=dev(x, y, (z + step) & 15, core), device_id_type=MESH)

    def hear(i):
        pl.semaphore_wait(line_sem.at[i], 2)

    tell(0)

    mine = pair * 2 + core

    half = z & 1

    def half_cols(h):
        return pl.ds(pl.multiple_of(h * BLOCK, BLOCK), BLOCK)

    def batch_rows(b):
        return pl.ds(pl.multiple_of(b * 64, 64), 64)

    def x_copy(view, dy, dlo):
        ty = (y + dy) & 3
        tlo = xlo ^ dlo
        tx = x if dlo == 0 else (x ^ 1 if view == 0 else 3 - x)
        src = (first, second)[view]
        if (dy, dlo) in WHOLE:
            col = pl.ds(pl.multiple_of((ty * 2 + tlo) * PAIR, PAIR), PAIR)
            there = xb.at[batch_rows(mine), :]
        else:
            col = pl.ds(pl.multiple_of((ty * 2 + tlo) * PAIR + half * BLOCK, BLOCK), BLOCK)
            there = xb.at[batch_rows(mine), half_cols(half)]
        return rcopy(
            src.at[:, col],
            there,
            x_s.at[(dy * 2 + dlo) * 2 + view],
            x_r.at[mine],
            dev(tx, ty, z, view),
        )

    def sib_copy(view):
        src = (first, second)[view]
        return rcopy(
            src.at[:, pl.ds(pl.multiple_of(pair * PAIR, PAIR), PAIR)],
            xb.at[batch_rows(mine), :],
            x_s.at[0],
            x_r.at[mine],
            sib,
        )

    def own_copy(view):
        src = (first, second)[view]
        return pltpu.make_async_copy(
            src.at[:, pl.ds(pl.multiple_of(pair * PAIR, PAIR), PAIR)],
            xb.at[batch_rows(mine), :],
            loc.at[0],
        )

    for dy, dlo in X_ORDER:
        for view in range(2):
            x_copy(view, dy, dlo).start()
    for view in range(2):
        @pl.when(core == view)
        def _():
            own_copy(view).start()

        @pl.when(core != view)
        def _():
            sib_copy(view).start()

    def x_sent():
        for dy, dlo in X_ORDER:
            for view in range(2):
                x_copy(view, dy, dlo).wait_send()
        for view in range(2):
            @pl.when(core != view)
            def _():
                sib_copy(view).wait_send()

    sent.append(x_sent)

    w_place = wb.at[pl.ds(pl.multiple_of(core * BLOCK, BLOCK), BLOCK), :]
    w_copy = rcopy(w, w_place, w_s, w_r, sib)
    w_copy.start()
    w_own = pltpu.make_async_copy(w, w_place, loc.at[1])
    w_own.start()
    w_own.wait()
    w_copy.wait()
    for i in range(PAIR // SLAB):
        wt[:, i * SLAB:(i + 1) * SLAB] = wb[i * SLAB:(i + 1) * SLAB, :].T
    def chunk_of(dy, dlo):
        return ((y + dy) & 3) * 2 + (xlo ^ dlo)

    def relay(dy, dlo, c):
        b = chunk_of(dy, dlo) * 2 + c
        place_there = xb.at[batch_rows(b), half_cols(half)]
        return rcopy(
            place_there, place_there, q_s.at[(dy * 2 + dlo) * 2 + c], q_r.at[b],
            dev(x, y, (z + (1 if c == 0 else 15)) & 15, core),
        )

    def product_of(chunk, h, add):
        rows = pl.ds(pl.multiple_of(chunk * 128, 128), 128)
        xs = xb[rows, half_cols(h)]
        part = lax.dot_general(wt[:, half_cols(h)], xs, ROW_DIMS, preferred_element_type=F32)
        pt[:, rows] = pt[:, rows] + part if add else part
        xt[half_cols(h), rows] = xs.T

    for dy, dlo in X_ORDER:
        for c in range(2):
            b = chunk_of(dy, dlo) * 2 + c
            if (dy, dlo) in WHOLE:
                got = xb.at[batch_rows(b), :]
                rcopy(got, got, x_s.at[0], x_r.at[b], sib).wait_recv()
            else:
                got = xb.at[batch_rows(b), half_cols(half)]
                rcopy(got, got, x_s.at[0], x_r.at[b], sib).wait_recv()
                relay(dy, dlo, c).start()
        product_of(chunk_of(dy, dlo), half, False)
        if (dy, dlo) in WHOLE:
            product_of(chunk_of(dy, dlo), 1 - half, True)

    relayed = [offset for offset in X_ORDER if offset not in WHOLE]

    def relay_sent():
        for dy, dlo in relayed:
            for c in range(2):
                relay(dy, dlo, c).wait_send()

    sent.append(relay_sent)

    for view in range(2):
        @pl.when(core == view)
        def _():
            own_copy(view).wait()
    got = xb.at[batch_rows(pair * 2 + 1 - core), :]
    rcopy(got, got, x_s.at[0], x_r.at[pair * 2 + 1 - core], sib).wait_recv()
    product_of(pair, half, False)
    product_of(pair, 1 - half, True)

    hear(0)
    tell(1)
    for dy, dlo in relayed:
        for c in range(2):
            b = chunk_of(dy, dlo) * 2 + c
            got = xb.at[batch_rows(b), half_cols(1 - half)]
            rcopy(got, got, q_s.at[0], q_r.at[b], sib).wait_recv()
        product_of(chunk_of(dy, dlo), 1 - half, True)

    def part_rows(part, p):
        return pl.ds(pl.multiple_of(part * HALF_SLAB + p * HALF_OWN, HALF_OWN), HALF_OWN)

    def rs_copy(k):
        i, part = k & 7, k >> 3
        ty = (y + (i >> 1)) & 3
        tlo = xlo ^ (i & 1)
        return rcopy(
            ptb.at[part_rows(part, ty * 2 + tlo), :], rsb.at[pair, part], rs_s.at[k], rs_r.at[part * PAIRS + pair],
            dev(xhi * 2 + tlo, ty, z, core),
        )

    def plane_rows(h, part, p):
        return pl.ds(pl.multiple_of(h * SLAB + part * HALF_SLAB + p * HALF_OWN, HALF_OWN), HALF_OWN)

    def ag_copy(k):
        part, h, dy = k >> 3, (k >> 2) & 1, k & 3
        return rcopy(
            ns.at[part_rows(part, pair), :], nt.at[plane_rows(xhi, part, pair), :], ag_s.at[k],
            ag_r.at[part * PAIRS + pair], dev(core + 2 * h, (y + dy) & 3, z, xhi),
        )

    alone = jnp.logical_and(core == xlo, core == xhi)

    def ag_far(part):
        return [part * 8 + h * 4 + dy for dy in (2, 1, 3, 0) for h in range(2)]

    def unless_mine(k, do):
        if k & 3 == 0:
            h = (k >> 2) & 1

            @pl.when(jnp.logical_not(jnp.logical_and(alone, xhi == h)))
            def _():
                do(ag_copy(k))
        else:
            do(ag_copy(k))

    def ag_sent():
        for k in range(16):
            unless_mine(k, lambda copy: copy.wait_send())

    sent.append(ag_sent)

    for part in range(2):
        for i in range(PAIRS):
            rows = slice(part * HALF_SLAB + i * HALF_OWN, part * HALF_SLAB + (i + 1) * HALF_OWN)
            values = pt[rows, :]
            ptb[rows, :] = (values - jnp.mean(values, 1, keepdims=True)).astype(BF)
        for i in GROUP_FAR:
            rs_copy(part * PAIRS + i).start()
        when_sent(rs_copy, [part * PAIRS + i for i in GROUP_FAR])

    hear(1)
    tell(2)
    scales = []
    for part in range(2):
        rsb[pair, part] = ptb[part_rows(part, pair), :]
        for i in GROUP_FAR:
            other = (pair + i) & 7
            got = rsb.at[other, part]
            rcopy(got, got, rs_s.at[0], rs_r.at[part * PAIRS + other], sib).wait_recv()
        total = rsb[0, part].astype(F32)
        for i in range(1, PAIRS):
            total = total + rsb[i, part].astype(F32)
        mean = jnp.sum(total, 1, keepdims=True) / ROWS
        spread = jnp.sum(total * total, 1, keepdims=True) / ROWS - mean * mean
        scales.append(lax.rsqrt(spread + 1e-05))
        normed = ((total - mean) * scales[part]).astype(BF)
        ns[part_rows(part, pair), :] = normed

        @pl.when(alone)
        def _():
            nt[plane_rows(xhi, part, pair), :] = normed

        for k in ag_far(part):
            unless_mine(k, lambda copy: copy.start())
    scale = jnp.concatenate(scales, 0)
    lane = lax.broadcasted_iota(jnp.int32, (8, 128), 1)
    wide = jnp.broadcast_to(scale, (OWN, 128))
    tile = wide[0:8]
    for i in range(1, OWN // 8):
        tile = jnp.where(lane >= 32 * i, wide[8 * i:8 * i + 8], tile)
    sc[pair] = tile

    def sc_copy(i):
        return rcopy(
            sc.at[pair], sc.at[pair], sc_s.at[i], sc_r.at[pair],
            dev(xhi * 2 + xlo ^ (i & 1), (y + (i >> 1)) & 3, z, core),
        )

    @each(GROUP_FAR)
    def _(i):
        sc_copy(i).start()

    when_sent(sc_copy, GROUP_FAR)

    strip_place = (y * 2 + xhi) * 2 + core
    lanes = pl.ds(pl.multiple_of((strip_place >> 1) * 128, 128), 128)

    def swap(part):
        rows = pl.ds(pl.multiple_of(core * SLAB + part * HALF_SLAB, HALF_SLAB), HALF_SLAB)
        return rcopy(nt.at[rows, :], nt.at[rows, :], sw_s.at[part], sw_r.at[part], sib)

    for part in range(2):
        for i in GROUP_FAR + [0]:
            other = (pair + i) & 7
            got = nt.at[plane_rows(core, part, other), :]

            def arrived():
                rcopy(got, got, ag_s.at[0], ag_r.at[part * PAIRS + other], sib).wait_recv()

            if i == 0:
                pl.when(jnp.logical_not(alone))(arrived)
            else:
                arrived()
        swap(part).start()
        swap(part).wait()
        for h in range(2):
            columns = slice(h * SLAB + part * HALF_SLAB, h * SLAB + (part + 1) * HALF_SLAB)
            kl[h] = nt[columns, lanes].T
            strip = kl[h, pl.ds(pl.multiple_of(core * STRIP, STRIP), STRIP), :]
            for i in range(4):
                cols = slice(i * 256, (i + 1) * 256)
                term = jnp.dot(strip, nt[columns, cols], preferred_element_type=F32)
                if part == 0 and h == 0:
                    ka[:, cols] = term
                elif part == 1 and h == 1:
                    kp[:, cols] = (ka[:, cols] + term).astype(BF)
                else:
                    ka[:, cols] += term

    @each(GROUP_FAR)
    def _(i):
        other = (pair + i) & 7
        rcopy(sc.at[other], sc.at[other], sc_s.at[0], sc_r.at[other], sib).wait_recv()

    hear(2)

    def piece(ref, t):
        return ref.at[pl.ds(pl.multiple_of((t >> 2) * 16, 16), 16), pl.ds(pl.multiple_of((t & 3) * 256, 256), 256)]

    def zr_copy(i):
        t = (z + i) & 15
        return rcopy(piece(kp, t), zb.at[z], zr_s.at[i], zr_r.at[z], dev(x, y, t, core))

    @each(LINE_FAR[:-1])
    def _(i):
        zr_copy(i).start()

    when_sent(zr_copy, LINE_FAR[:-1])

    def ns_copy(k):
        i, part = k & 7, k >> 3
        rows = part_rows(part, pair)
        return rcopy(
            ns.at[rows, :], ns.at[rows, :], ns_s.at[k], ns_r.at[part * PAIRS + pair],
            dev(xhi * 2 + (xlo ^ (i & 1)), (y + (i >> 1)) & 3, z, core),
        )

    ns_all = [part * PAIRS + i for i in GROUP_FAR for part in range(2)]
    for k in ns_all:
        ns_copy(k).start()
    when_sent(ns_copy, ns_all)

    zb[z] = kp[
        pl.ds(pl.multiple_of((z >> 2) * 16, 16), 16), pl.ds(pl.multiple_of((z & 3) * 256, 256), 256)
    ]

    @each(LINE_FAR[:-1])
    def _(i):
        t = (z + i) & 15
        rcopy(zb.at[t], zb.at[t], zr_s.at[0], zr_r.at[t], sib).wait_recv()

    acc = zb[0].astype(F32)
    for i in range(1, NZ):
        acc = acc + zb[i].astype(F32)
    ks[...] = acc.astype(BF)

    def za_copy(i):
        return rcopy(ks, piece(kf, z), za_s.at[i], za_r.at[z], dev(x ^ 1, y, (z + i) & 15, core))

    @each(LINE_FAR)
    def _(i):
        za_copy(i).start()

    when_sent(za_copy, LINE_FAR)

    for k in ns_all:
        i, part = k & 7, k >> 3
        other = (pair + i) & 7
        got = ns.at[part_rows(part, other), :]
        rcopy(got, got, ns_s.at[0], ns_r.at[part * PAIRS + other], sib).wait_recv()
    n_copy = rcopy(ns, noth, n_s, n_r, sib)
    n_copy.start()
    for i in range(8):
        rows = slice(i * 128, (i + 1) * 128)
        nn[rows, :] = ns[:, rows].T
    n_copy.wait()
    for i in range(8):
        rows = slice(i * 128, (i + 1) * 128)
        no[rows, :] = noth[:, rows].T
    diag = jnp.zeros((1, SLAB), F32)
    for i in range(8):
        rows = slice(i * 128, (i + 1) * 128)
        diag = diag + jnp.sum(nn[rows, :].astype(F32) * no[rows, :].astype(F32), 0, keepdims=True)
    diag = diag / ROWS
    d = -2.0 * (1.0 - diag) - 2.0 * off_weight * diag

    cols = []
    for part in range(2):
        for i in range(PAIRS):
            t = sc[i]
            for j in (2 * part, 2 * part + 1):
                cols.append(jnp.broadcast_to(t[:, 32 * j:32 * j + 1], (8, 128)))
    scale_row = jnp.concatenate(cols, 0).T[0:1, :]

    for i in LINE_FAR:
        t = (z + i) & 15
        rcopy(ks, piece(kf, t), za_s.at[0], za_r.at[t], sib).wait_recv()

    def g_rows(s):
        return pl.ds(pl.multiple_of(s * STRIP, STRIP), STRIP)

    def g_copy(i):
        tx = (x + i) & 3
        return rcopy(
            gs.at[tx >> 1], gb.at[g_rows(strip_place), :], g_s.at[i], g_r.at[strip_place],
            dev(tx, (y + (i >> 2)) & 3, z, xlo),
        )

    for h in range(2):
        gs[h] = lax.dot_general(
            kf[...], nt[h * SLAB:(h + 1) * SLAB, :], ROW_DIMS, preferred_element_type=F32
        ).astype(BF)
    for i in PLANE_FAR:
        g_copy(i).start()

    @pl.when(core == xlo)
    def _():
        gb[g_rows(strip_place), :] = gs[xhi]

    @pl.when(core != xlo)
    def _():
        g_copy(0).start()

    def g_sent():
        for i in PLANE_FAR:
            g_copy(i).wait_send()

        @pl.when(core != xlo)
        def _():
            g_copy(0).wait_send()

    sent.append(g_sent)

    for s in range(16):
        def arrived():
            got = gb.at[g_rows(s), :]
            rcopy(got, got, g_s.at[0], g_r.at[s], sib).wait_recv()

        pl.when(jnp.logical_or(core != xlo, strip_place != s))(arrived)

    g_sum = jnp.zeros((1, SLAB), F32)
    gn_sum = jnp.zeros((1, SLAB), F32)
    for i in range(8):
        rows = slice(i * 128, (i + 1) * 128)
        g = gb[rows, :].astype(F32) * (2.0 * off_weight / ROWS) + no[rows, :].astype(F32) * d
        gw[rows, :] = g
        g_sum = g_sum + jnp.sum(g, 0, keepdims=True)
        gn_sum = gn_sum + jnp.sum(g * nn[rows, :].astype(F32), 0, keepdims=True)
    g_mean = g_sum / ROWS
    gn_mean = gn_sum / ROWS
    for i in range(8):
        rows = slice(i * 128, (i + 1) * 128)
        cb[rows, :] = (gw[rows, :] - g_mean - nn[rows, :].astype(F32) * gn_mean).astype(BF)

    factor = scale_row * (64.0 / ROWS)

    def product(block, i):
        rows = pl.ds(pl.multiple_of(block * BLOCK + i * 128, 128), 128)
        return jnp.dot(xt[rows, :], cb[...], preferred_element_type=F32) * factor

    def f_copy(i):
        rows = pl.ds(i * 128, 128)
        return rcopy(fs.at[rows, :], fr.at[rows, :], f_s.at[i], f_r.at[i], sib)

    for i in range(4):
        fs[i * 128:(i + 1) * 128, :] = product(1 - core, i)
        f_copy(i).start()
    when_sent(f_copy, range(4))
    for i in range(4):
        rows = slice(i * 128, (i + 1) * 128)
        part = product(core, i)
        f_copy(i).wait_recv()
        out[rows, :] = part + fr[rows, :]

    for wait in sent:
        wait()


def local(first_view, second_view, weight):
    dma = pltpu.SemaphoreType.DMA
    vm = pltpu.VMEM
    return pl.pallas_call(
        kernel,
        out_shape=jax.ShapeDtypeStruct((BLOCK, SLAB), F32),
        in_specs=[pl.BlockSpec(memory_space=pl.ANY)] * 3,
        out_specs=pl.BlockSpec(memory_space=pltpu.VMEM),
        scratch_shapes=[
            vm((ROWS, PAIR), BF), vm((PAIR, ROWS), BF), vm((PAIR, SLAB), BF), vm((SLAB, PAIR), BF),
            vm((SLAB, ROWS), F32), vm((SLAB, ROWS), BF), vm((PAIRS, 2, HALF_OWN, ROWS), BF), vm((2 * SLAB, ROWS), BF),
            vm((PAIRS, 8, 128), F32), vm((8, 128), F32), vm((SLAB, ROWS), BF), vm((2, 128, HALF_SLAB), BF),
            vm((STRIP, ROWS), BF), vm((NZ, 16, 256), BF), vm((16, 256), BF), vm((STRIP, ROWS), BF),
            vm((2, STRIP, SLAB), BF), vm((ROWS, SLAB), BF), vm((ROWS, SLAB), BF), vm((ROWS, SLAB), BF),
            vm((ROWS, SLAB), F32), vm((ROWS, SLAB), BF), vm((BLOCK, SLAB), F32), vm((BLOCK, SLAB), F32),
            dma((2,)), dma((16,)), dma((16,)), dma((16,)), dma((16,)), dma, dma, dma((16,)), dma((16,)), dma((16,)), dma((16,)),
            dma((PAIRS,)), dma((PAIRS,)), dma, dma, dma((NZ,)), dma((NZ,)), dma((NZ,)), dma((NZ,)),
            dma((16,)), dma((16,)), dma((4,)), dma((4,)),
            dma((2,)), dma((2,)), dma((16,)), dma((16,)), vm((SLAB, ROWS), BF), vm((STRIP, ROWS), F32),
            pltpu.SemaphoreType.REGULAR((3,)),
        ],
        compiler_params=pltpu.CompilerParams(collective_id=0, has_side_effects=True, vmem_limit_bytes=53 << 20),
        cost_estimate=pl.CostEstimate(flops=4 * 10**9, bytes_accessed=4 << 20, transcendentals=0),
    )(first_view, second_view, weight)


def solution(mesh):
    return jax.shard_map(
        local,
        mesh=mesh,
        in_specs=(P("batch", None), P("batch", None), P("batch", "feat")),
        out_specs=P("batch", "feat"),
        check_vma=False,
    )
```

```python
import functools

import jax
import jax.numpy as jnp
from jax import lax
from jax.experimental import pallas as pl
from jax.experimental.pallas import tpu as pltpu
from jax.sharding import PartitionSpec as P

MESH = pl.DeviceIdType.MESH
off_weight = 0.0051
NX, NY, NZ = 4, 4, 16
ROWS = 1024
BLOCK = 512
SLAB = 256
PAIR = 2 * BLOCK
PAIRS = 8
OWN = SLAB // PAIRS
HALF_OWN = OWN // 2
HALF_SLAB = SLAB // 2
STRIP = ROWS // (NX * NY)
BF = jnp.bfloat16
F32 = jnp.float32

ROW_DIMS = (((1,), (1,)), ((), ()))


def coords():
    b = lax.axis_index("batch")
    f = lax.axis_index("feat")
    return (f & 1) * 2 + ((b >> 1) & 1), b >> 2, f >> 1, b & 1


def dev(x, y, z, core):
    return (y * 4 + (x & 1) * 2 + core, z * 2 + (x >> 1))


def each(values):
    def run(body):
        for i in values:
            body(i)

    return run


def ring(step, size):
    return min(step, size - step)


PLANE_FAR = sorted(range(1, 16), key=lambda i: -ring(i & 3, 4) - ring(i >> 2, 4))
GROUP_FAR = sorted(range(1, PAIRS), key=lambda i: -(i & 1) - ring(i >> 1, 4))
X_ORDER = [(1, 1), (3, 1), (1, 0), (3, 0), (2, 1), (2, 0), (0, 1)]
WHOLE = [(0, 1)]
LINE_FAR = sorted(range(NZ), key=lambda i: -ring(i, NZ))


def rcopy(src, dst, send, recv, device):
    return pltpu.make_async_remote_copy(
        src_ref=src, dst_ref=dst, send_sem=send, recv_sem=recv, device_id=device, device_id_type=MESH
    )


def kernel(
    first, second, w, out,
    xb, xt, wb, wt, pt, ptb, rsb, nt, sc, scb, noth, kl, kp, zb, ks, kf, gs, gb, nn, no, gw, cb, fs, fr,
    loc, x_s, x_r, q_s, q_r, w_s, w_r, rs_s, rs_r, ag_s, ag_r, sc_s, sc_r, n_s, n_r, zr_s, zr_r, za_s, za_r, g_s, g_r, f_s, f_r,
    sw_s, sw_r, ns_s, ns_r, ns, ka, line_sem,
):
    x, y, z, core = coords()
    xlo, xhi = x & 1, x >> 1
    pair = y * 2 + xlo
    place = y * NX + x
    sib = dev(x, y, z, 1 - core)
    sent = []

    def when_sent(copy, values):
        def wait():
            for i in values:
                copy(i).wait_send()

        sent.append(wait)

    barrier = pltpu.get_barrier_semaphore()
    pl.semaphore_signal(barrier, 1, device_id=sib, device_id_type=MESH)

    @each(PLANE_FAR)
    def _(i):
        for c in range(2):
            pl.semaphore_signal(
                barrier, 1, device_id=dev((x + i) & 3, (y + (i >> 2)) & 3, z, c), device_id_type=MESH
            )

    for i in (1, NZ - 1):
        for c in range(2):
            pl.semaphore_signal(barrier, 1, device_id=dev(x ^ c, y, (z + i) & 15, core), device_id_type=MESH)

    pl.semaphore_wait(barrier, 1 + 2 * (NX * NY - 1) + 4)

    def tell(i):
        for step in (1 << i, NZ - (1 << i)):
            pl.semaphore_signal(line_sem.at[i], 1, device_id=dev(x, y, (z + step) & 15, core), device_id_type=MESH)

    def hear(i):
        pl.semaphore_wait(line_sem.at[i], 2)

    tell(0)

    mine = pair * 2 + core

    half = z & 1

    def half_cols(h):
        return pl.ds(pl.multiple_of(h * BLOCK, BLOCK), BLOCK)

    def batch_rows(b):
        return pl.ds(pl.multiple_of(b * 64, 64), 64)

    def x_copy(view, dy, dlo):
        ty = (y + dy) & 3
        tlo = xlo ^ dlo
        tx = x if dlo == 0 else (x ^ 1 if view == 0 else 3 - x)
        src = (first, second)[view]
        if (dy, dlo) in WHOLE:
            col = pl.ds(pl.multiple_of((ty * 2 + tlo) * PAIR, PAIR), PAIR)
            there = xb.at[batch_rows(mine), :]
        else:
            col = pl.ds(pl.multiple_of((ty * 2 + tlo) * PAIR + half * BLOCK, BLOCK), BLOCK)
            there = xb.at[batch_rows(mine), half_cols(half)]
        return rcopy(
            src.at[:, col],
            there,
            x_s.at[(dy * 2 + dlo) * 2 + view],
            x_r.at[mine],
            dev(tx, ty, z, view),
        )

    def sib_copy(view):
        src = (first, second)[view]
        return rcopy(
            src.at[:, pl.ds(pl.multiple_of(pair * PAIR, PAIR), PAIR)],
            xb.at[batch_rows(mine), :],
            x_s.at[0],
            x_r.at[mine],
            sib,
        )

    def own_copy(view):
        src = (first, second)[view]
        return pltpu.make_async_copy(
            src.at[:, pl.ds(pl.multiple_of(pair * PAIR, PAIR), PAIR)],
            xb.at[batch_rows(mine), :],
            loc.at[0],
        )

    for dy, dlo in X_ORDER:
        for view in range(2):
            x_copy(view, dy, dlo).start()
    for view in range(2):
        @pl.when(core == view)
        def _():
            own_copy(view).start()

        @pl.when(core != view)
        def _():
            sib_copy(view).start()

    def x_sent():
        for dy, dlo in X_ORDER:
            for view in range(2):
                x_copy(view, dy, dlo).wait_send()
        for view in range(2):
            @pl.when(core != view)
            def _():
                sib_copy(view).wait_send()

    sent.append(x_sent)

    w_place = wb.at[pl.ds(pl.multiple_of(core * BLOCK, BLOCK), BLOCK), :]
    w_copy = rcopy(w, w_place, w_s, w_r, sib)
    w_copy.start()
    w_own = pltpu.make_async_copy(w, w_place, loc.at[1])
    w_own.start()
    w_own.wait()
    w_copy.wait()
    for i in range(PAIR // SLAB):
        wt[:, i * SLAB:(i + 1) * SLAB] = wb[i * SLAB:(i + 1) * SLAB, :].T
    def chunk_of(dy, dlo):
        return ((y + dy) & 3) * 2 + (xlo ^ dlo)

    def relay(dy, dlo, c):
        b = chunk_of(dy, dlo) * 2 + c
        place_there = xb.at[batch_rows(b), half_cols(half)]
        return rcopy(
            place_there, place_there, q_s.at[(dy * 2 + dlo) * 2 + c], q_r.at[b],
            dev(x, y, (z + (1 if c == 0 else 15)) & 15, core),
        )

    def product_of(chunk, h, add):
        rows = pl.ds(pl.multiple_of(chunk * 128, 128), 128)
        xs = xb[rows, half_cols(h)]
        part = lax.dot_general(wt[:, half_cols(h)], xs, ROW_DIMS, preferred_element_type=F32)
        pt[:, rows] = pt[:, rows] + part if add else part
        if not add:
            xt[half_cols(h), rows] = xs.T

    for dy, dlo in X_ORDER:
        for c in range(2):
            b = chunk_of(dy, dlo) * 2 + c
            if (dy, dlo) in WHOLE:
                got = xb.at[batch_rows(b), :]
                rcopy(got, got, x_s.at[0], x_r.at[b], sib).wait_recv()
            else:
                got = xb.at[batch_rows(b), half_cols(half)]
                rcopy(got, got, x_s.at[0], x_r.at[b], sib).wait_recv()
                relay(dy, dlo, c).start()
        product_of(chunk_of(dy, dlo), half, False)
        if (dy, dlo) in WHOLE:
            product_of(chunk_of(dy, dlo), 1 - half, True)

    relayed = [offset for offset in X_ORDER if offset not in WHOLE]

    def relay_sent():
        for dy, dlo in relayed:
            for c in range(2):
                relay(dy, dlo, c).wait_send()

    sent.append(relay_sent)

    for view in range(2):
        @pl.when(core == view)
        def _():
            own_copy(view).wait()
    got = xb.at[batch_rows(pair * 2 + 1 - core), :]
    rcopy(got, got, x_s.at[0], x_r.at[pair * 2 + 1 - core], sib).wait_recv()
    product_of(pair, half, False)
    product_of(pair, 1 - half, True)

    hear(0)
    tell(1)
    for dy, dlo in relayed:
        for c in range(2):
            b = chunk_of(dy, dlo) * 2 + c
            got = xb.at[batch_rows(b), half_cols(1 - half)]
            rcopy(got, got, q_s.at[0], q_r.at[b], sib).wait_recv()
        product_of(chunk_of(dy, dlo), 1 - half, True)

    def part_rows(part, p):
        return pl.ds(pl.multiple_of(part * HALF_SLAB + p * HALF_OWN, HALF_OWN), HALF_OWN)

    def rs_copy(k):
        i, part = k & 7, k >> 3
        ty = (y + (i >> 1)) & 3
        tlo = xlo ^ (i & 1)
        return rcopy(
            ptb.at[part_rows(part, ty * 2 + tlo), :], rsb.at[pair, part], rs_s.at[k], rs_r.at[part * PAIRS + pair],
            dev(xhi * 2 + tlo, ty, z, core),
        )

    def plane_rows(h, part, p):
        return pl.ds(pl.multiple_of(h * SLAB + part * HALF_SLAB + p * HALF_OWN, HALF_OWN), HALF_OWN)

    def ag_copy(k):
        part, h, dy = k >> 3, (k >> 2) & 1, k & 3
        return rcopy(
            ns.at[part_rows(part, pair), :], nt.at[plane_rows(xhi, part, pair), :], ag_s.at[k],
            ag_r.at[part * PAIRS + pair], dev(core + 2 * h, (y + dy) & 3, z, xhi),
        )

    alone = jnp.logical_and(core == xlo, core == xhi)

    def ag_far(part):
        return [part * 8 + h * 4 + dy for dy in (2, 1, 3, 0) for h in range(2)]

    def unless_mine(k, do):
        if k & 3 == 0:
            h = (k >> 2) & 1

            @pl.when(jnp.logical_not(jnp.logical_and(alone, xhi == h)))
            def _():
                do(ag_copy(k))
        else:
            do(ag_copy(k))

    def ag_sent():
        for k in range(16):
            unless_mine(k, lambda copy: copy.wait_send())

    sent.append(ag_sent)

    for part in range(2):
        for i in range(PAIRS):
            rows = slice(part * HALF_SLAB + i * HALF_OWN, part * HALF_SLAB + (i + 1) * HALF_OWN)
            values = pt[rows, :]
            ptb[rows, :] = (values - jnp.mean(values, 1, keepdims=True)).astype(BF)
        for i in GROUP_FAR:
            rs_copy(part * PAIRS + i).start()
        when_sent(rs_copy, [part * PAIRS + i for i in GROUP_FAR])

    hear(1)
    tell(2)
    scales = []
    for part in range(2):
        rsb[pair, part] = ptb[part_rows(part, pair), :]
        for i in GROUP_FAR:
            other = (pair + i) & 7
            got = rsb.at[other, part]
            rcopy(got, got, rs_s.at[0], rs_r.at[part * PAIRS + other], sib).wait_recv()
        total = rsb[0, part].astype(F32)
        for i in range(1, PAIRS):
            total = total + rsb[i, part].astype(F32)
        mean = jnp.sum(total, 1, keepdims=True) / ROWS
        spread = jnp.sum(total * total, 1, keepdims=True) / ROWS - mean * mean
        scales.append(lax.rsqrt(spread + 1e-05))
        normed = ((total - mean) * scales[part]).astype(BF)
        ns[part_rows(part, pair), :] = normed

        @pl.when(alone)
        def _():
            nt[plane_rows(xhi, part, pair), :] = normed

        for k in ag_far(part):
            unless_mine(k, lambda copy: copy.start())
    scale = jnp.concatenate(scales, 0)
    lane = lax.broadcasted_iota(jnp.int32, (8, 128), 1)
    wide = jnp.broadcast_to(scale, (OWN, 128))
    tile = wide[0:8]
    for i in range(1, OWN // 8):
        tile = jnp.where(lane >= 32 * i, wide[8 * i:8 * i + 8], tile)
    sc[pair] = tile

    def sc_copy(i):
        return rcopy(
            sc.at[pair], sc.at[pair], sc_s.at[i], sc_r.at[pair],
            dev(xhi * 2 + xlo ^ (i & 1), (y + (i >> 1)) & 3, z, core),
        )

    @each(GROUP_FAR)
    def _(i):
        sc_copy(i).start()

    when_sent(sc_copy, GROUP_FAR)

    strip_place = (y * 2 + xhi) * 2 + core
    lanes = pl.ds(pl.multiple_of((strip_place >> 1) * 128, 128), 128)

    def swap(part):
        rows = pl.ds(pl.multiple_of(core * SLAB + part * HALF_SLAB, HALF_SLAB), HALF_SLAB)
        return rcopy(nt.at[rows, :], nt.at[rows, :], sw_s.at[part], sw_r.at[part], sib)

    for part in range(2):
        for i in GROUP_FAR + [0]:
            other = (pair + i) & 7
            got = nt.at[plane_rows(core, part, other), :]

            def arrived():
                rcopy(got, got, ag_s.at[0], ag_r.at[part * PAIRS + other], sib).wait_recv()

            if i == 0:
                pl.when(jnp.logical_not(alone))(arrived)
            else:
                arrived()
        swap(part).start()
        swap(part).wait()
        for h in range(2):
            columns = slice(h * SLAB + part * HALF_SLAB, h * SLAB + (part + 1) * HALF_SLAB)
            kl[h] = nt[columns, lanes].T
            strip = kl[h, pl.ds(pl.multiple_of(core * STRIP, STRIP), STRIP), :]
            for i in range(4):
                cols = slice(i * 256, (i + 1) * 256)
                term = jnp.dot(strip, nt[columns, cols], preferred_element_type=F32)
                if part == 0 and h == 0:
                    ka[:, cols] = term
                elif part == 1 and h == 1:
                    kp[:, cols] = (ka[:, cols] + term).astype(BF)
                else:
                    ka[:, cols] += term

    @each(GROUP_FAR)
    def _(i):
        other = (pair + i) & 7
        rcopy(sc.at[other], sc.at[other], sc_s.at[0], sc_r.at[other], sib).wait_recv()

    hear(2)

    def piece(ref, t):
        return ref.at[pl.ds(pl.multiple_of((t >> 2) * 16, 16), 16), pl.ds(pl.multiple_of((t & 3) * 256, 256), 256)]

    def zr_copy(i):
        t = (z + i) & 15
        return rcopy(piece(kp, t), zb.at[z], zr_s.at[i], zr_r.at[z], dev(x, y, t, core))

    @each(LINE_FAR[:-1])
    def _(i):
        zr_copy(i).start()

    when_sent(zr_copy, LINE_FAR[:-1])

    def ns_copy(k):
        i, part = k & 7, k >> 3
        rows = part_rows(part, pair)
        return rcopy(
            ns.at[rows, :], ns.at[rows, :], ns_s.at[k], ns_r.at[part * PAIRS + pair],
            dev(xhi * 2 + (xlo ^ (i & 1)), (y + (i >> 1)) & 3, z, core),
        )

    ns_all = [part * PAIRS + i for i in GROUP_FAR for part in range(2)]
    for k in ns_all:
        ns_copy(k).start()
    when_sent(ns_copy, ns_all)

    for i in range(ROWS // 128):
        rows = slice(i * 128, (i + 1) * 128)
        xt[half_cols(1 - half), rows] = xb[rows, half_cols(1 - half)].T

    zb[z] = kp[
        pl.ds(pl.multiple_of((z >> 2) * 16, 16), 16), pl.ds(pl.multiple_of((z & 3) * 256, 256), 256)
    ]

    @each(LINE_FAR[:-1])
    def _(i):
        t = (z + i) & 15
        rcopy(zb.at[t], zb.at[t], zr_s.at[0], zr_r.at[t], sib).wait_recv()

    acc = zb[0].astype(F32)
    for i in range(1, NZ):
        acc = acc + zb[i].astype(F32)
    ks[...] = acc.astype(BF)

    def za_copy(i):
        return rcopy(ks, piece(kf, z), za_s.at[i], za_r.at[z], dev(x ^ 1, y, (z + i) & 15, core))

    @each(LINE_FAR)
    def _(i):
        za_copy(i).start()

    when_sent(za_copy, LINE_FAR)

    for k in ns_all:
        i, part = k & 7, k >> 3
        other = (pair + i) & 7
        got = ns.at[part_rows(part, other), :]
        rcopy(got, got, ns_s.at[0], ns_r.at[part * PAIRS + other], sib).wait_recv()
    n_copy = rcopy(ns, noth, n_s, n_r, sib)
    n_copy.start()
    for i in range(8):
        rows = slice(i * 128, (i + 1) * 128)
        nn[rows, :] = ns[:, rows].T
    n_copy.wait()
    for i in range(8):
        rows = slice(i * 128, (i + 1) * 128)
        no[rows, :] = noth[:, rows].T
    diag = jnp.zeros((1, SLAB), F32)
    for i in range(8):
        rows = slice(i * 128, (i + 1) * 128)
        diag = diag + jnp.sum(nn[rows, :].astype(F32) * no[rows, :].astype(F32), 0, keepdims=True)
    diag = diag / ROWS
    d = -2.0 * (1.0 - diag) - 2.0 * off_weight * diag

    cols = []
    for part in range(2):
        for i in range(PAIRS):
            t = sc[i]
            for j in (2 * part, 2 * part + 1):
                cols.append(jnp.broadcast_to(t[:, 32 * j:32 * j + 1], (8, 128)))
    scale_row = jnp.concatenate(cols, 0).T[0:1, :]

    for i in LINE_FAR:
        t = (z + i) & 15
        rcopy(ks, piece(kf, t), za_s.at[0], za_r.at[t], sib).wait_recv()

    def g_rows(s):
        return pl.ds(pl.multiple_of(s * STRIP, STRIP), STRIP)

    def g_copy(i):
        tx = (x + i) & 3
        return rcopy(
            gs.at[tx >> 1], gb.at[g_rows(strip_place), :], g_s.at[i], g_r.at[strip_place],
            dev(tx, (y + (i >> 2)) & 3, z, xlo),
        )

    for h in range(2):
        gs[h] = lax.dot_general(
            kf[...], nt[h * SLAB:(h + 1) * SLAB, :], ROW_DIMS, preferred_element_type=F32
        ).astype(BF)
    for i in PLANE_FAR:
        g_copy(i).start()

    @pl.when(core == xlo)
    def _():
        gb[g_rows(strip_place), :] = gs[xhi]

    @pl.when(core != xlo)
    def _():
        g_copy(0).start()

    def g_sent():
        for i in PLANE_FAR:
            g_copy(i).wait_send()

        @pl.when(core != xlo)
        def _():
            g_copy(0).wait_send()

    sent.append(g_sent)

    for s in range(16):
        def arrived():
            got = gb.at[g_rows(s), :]
            rcopy(got, got, g_s.at[0], g_r.at[s], sib).wait_recv()

        pl.when(jnp.logical_or(core != xlo, strip_place != s))(arrived)

    g_sum = jnp.zeros((1, SLAB), F32)
    gn_sum = jnp.zeros((1, SLAB), F32)
    for i in range(8):
        rows = slice(i * 128, (i + 1) * 128)
        g = gb[rows, :].astype(F32) * (2.0 * off_weight / ROWS) + no[rows, :].astype(F32) * d
        gw[rows, :] = g
        g_sum = g_sum + jnp.sum(g, 0, keepdims=True)
        gn_sum = gn_sum + jnp.sum(g * nn[rows, :].astype(F32), 0, keepdims=True)
    g_mean = g_sum / ROWS
    gn_mean = gn_sum / ROWS
    for i in range(8):
        rows = slice(i * 128, (i + 1) * 128)
        cb[rows, :] = (gw[rows, :] - g_mean - nn[rows, :].astype(F32) * gn_mean).astype(BF)

    factor = scale_row * (64.0 / ROWS)

    def product(block, i):
        rows = pl.ds(pl.multiple_of(block * BLOCK + i * 128, 128), 128)
        return jnp.dot(xt[rows, :], cb[...], preferred_element_type=F32) * factor

    def f_copy(i):
        rows = pl.ds(i * 128, 128)
        return rcopy(fs.at[rows, :], fr.at[rows, :], f_s.at[i], f_r.at[i], sib)

    for i in range(4):
        fs[i * 128:(i + 1) * 128, :] = product(1 - core, i)
        f_copy(i).start()
    when_sent(f_copy, range(4))
    for i in range(4):
        rows = slice(i * 128, (i + 1) * 128)
        part = product(core, i)
        f_copy(i).wait_recv()
        out[rows, :] = part + fr[rows, :]

    for wait in sent:
        wait()


def local(first_view, second_view, weight):
    dma = pltpu.SemaphoreType.DMA
    vm = pltpu.VMEM
    return pl.pallas_call(
        kernel,
        out_shape=jax.ShapeDtypeStruct((BLOCK, SLAB), F32),
        in_specs=[pl.BlockSpec(memory_space=pl.ANY)] * 3,
        out_specs=pl.BlockSpec(memory_space=pltpu.VMEM),
        scratch_shapes=[
            vm((ROWS, PAIR), BF), vm((PAIR, ROWS), BF), vm((PAIR, SLAB), BF), vm((SLAB, PAIR), BF),
            vm((SLAB, ROWS), F32), vm((SLAB, ROWS), BF), vm((PAIRS, 2, HALF_OWN, ROWS), BF), vm((2 * SLAB, ROWS), BF),
            vm((PAIRS, 8, 128), F32), vm((8, 128), F32), vm((SLAB, ROWS), BF), vm((2, 128, HALF_SLAB), BF),
            vm((STRIP, ROWS), BF), vm((NZ, 16, 256), BF), vm((16, 256), BF), vm((STRIP, ROWS), BF),
            vm((2, STRIP, SLAB), BF), vm((ROWS, SLAB), BF), vm((ROWS, SLAB), BF), vm((ROWS, SLAB), BF),
            vm((ROWS, SLAB), F32), vm((ROWS, SLAB), BF), vm((BLOCK, SLAB), F32), vm((BLOCK, SLAB), F32),
            dma((2,)), dma((16,)), dma((16,)), dma((16,)), dma((16,)), dma, dma, dma((16,)), dma((16,)), dma((16,)), dma((16,)),
            dma((PAIRS,)), dma((PAIRS,)), dma, dma, dma((NZ,)), dma((NZ,)), dma((NZ,)), dma((NZ,)),
            dma((16,)), dma((16,)), dma((4,)), dma((4,)),
            dma((2,)), dma((2,)), dma((16,)), dma((16,)), vm((SLAB, ROWS), BF), vm((STRIP, ROWS), F32),
            pltpu.SemaphoreType.REGULAR((3,)),
        ],
        compiler_params=pltpu.CompilerParams(collective_id=0, has_side_effects=True, vmem_limit_bytes=53 << 20),
        cost_estimate=pl.CostEstimate(flops=4 * 10**9, bytes_accessed=4 << 20, transcendentals=0),
    )(first_view, second_view, weight)


def solution(mesh):
    return jax.shard_map(
        local,
        mesh=mesh,
        in_specs=(P("batch", None), P("batch", None), P("batch", "feat")),
        out_specs=P("batch", "feat"),
        check_vma=False,
    )
```
